256 devices in a mesh: band: 128 (over y_lo, z, x, core), grid: 2 (over y_hi).
Axes of the slice: x: 4, y: 4 (y_hi: 2, y_lo: 2; y = y_hi * 2 + y_lo), z: 8, core: 2. Of those that a mesh axis runs over, the one named last changes fastest.
Arguments:
- orbitals: float32 [128, 80, 80, 80], P('band', 'grid'), may hold values from -6 to 6
Outputs:
- exchange_field: float32 [128, 80, 80, 80], P('band', 'grid')
The draws below stay inside these ranges and needn't reach their ends.
All inputs are finite; a program needn't handle non-finite values.
Results may differ from the reference program's by a relative error of at most 0.0003.
Values sent between devices are 32-bit elements; how exact they have to be, the bound alone decides.
No kernel may reach another device: no remote copies, remote signals or barrier semaphores. Data moves between devices by JAX's collectives and lax.ppermute only.
A program may use at most 64 MiB of HBM per device.

```python
import math
import jax
import jax.numpy as jnp
from jax import lax

ORB_DEV = 1
NX = 80
NY = 80
NZ = 80
STEPS = 3
ORBS = 128
N_BAND = 128


def levels(own_key, dims, split, smallest, top_value):
    level, own = 1.0, jax.random.fold_in(own_key, 6)
    for position, parts in split:
        draws = jnp.exp(jax.random.uniform(jax.random.fold_in(own, position), (parts,), jnp.float32, smallest / len(split), top_value / len(split)))
        level = level * jnp.repeat(draws, dims[position] // parts).reshape([-1 if axis == position else 1 for axis in range(len(dims))])
    return level


def normal_values(key, dims, spread, limit, split=(), held_as=jnp.bfloat16):
    level = levels(key, dims, split, -0.22, 0.18) if split else 1.0
    array = jax.random.normal(key, dims, jnp.float32) * spread * level
    return jnp.minimum(jnp.maximum(array, -limit), limit).astype(held_as)


def setup_inputs(seed: int = 0) -> dict:
    seeds = jax.random.split(jax.random.key(seed), 2)
    return {
        "orbitals": normal_values(seeds[0], (ORBS, NX, NY, NZ), 1.0, 6.0, ((0, 128), (1, 2)), jnp.float32),
    }


CELL_LENGTH = 37.2
SCREENING = 0.106


def frequencies(points):
    positions = jnp.arange(points, dtype=jnp.int32)
    return jnp.where(2 * positions >= points, positions - points, positions)


def screened_kernel(freq_x, freq_y, freq_z):
    squares = (freq_x * freq_x + freq_y * freq_y + freq_z * freq_z).astype(jnp.float32)
    wave_square = squares * (2.0 * math.pi / CELL_LENGTH) ** 2
    safe_square = jnp.where(squares == 0, 1.0, wave_square)
    shaped = 4.0 * math.pi / safe_square * (1.0 - jnp.exp(-safe_square / (4.0 * SCREENING ** 2)))
    return jnp.where(squares == 0, math.pi / SCREENING ** 2, shaped)


def reference(orbitals):
    kernel = screened_kernel(frequencies(NX)[:, None, None], frequencies(NY)[None, :, None], frequencies(NZ)[None, None, :])
    blocks = orbitals.reshape(N_BAND, ORB_DEV, NX, NY, NZ)

    def coulomb(density):
        spectrum = jnp.fft.fftn(density, axes=(-3, -2, -1))
        return jnp.real(jnp.fft.ifftn(spectrum * kernel, axes=(-3, -2, -1))).astype(jnp.float32)

    summed = jnp.zeros_like(blocks)
    for offset in range(1, STEPS + 1):
        def block_terms(device):
            resident = blocks[device]
            visitor = blocks[(device - offset) % N_BAND]
            potential = coulomb(resident[:, None] * visitor[None, :])
            return jnp.sum(visitor[None, :] * potential, axis=1), jnp.sum(resident[:, None] * potential, axis=0)

        own_sum, away_sum = lax.map(block_terms, jnp.arange(N_BAND, dtype=jnp.int32))
        summed = summed + own_sum + jnp.roll(away_sum, -offset, axis=0)
    return summed.reshape(ORBS, NX, NY, NZ)
```

```python
import functools
import math

import jax
import jax.numpy as jnp
import numpy as np
from jax import lax
from jax.experimental import pallas as pl
from jax.experimental.pallas import tpu as pltpu
from jax.sharding import PartitionSpec as P

CELL_LENGTH = 37.2
SCREENING = 0.106
BF16 = jnp.bfloat16
F32 = jnp.float32
N = 80
HALF = N // 2
GROUP = 8
GROUPS = HALF // GROUP
PLANES = 5
PACKED = (GROUPS * PLANES, N, 128)
LANES = 128
LOW, HIGH = 64, 16

FOLD = np.concatenate([np.arange(HALF), [HALF], np.arange(N - 1, HALF, -1)])


def cas(rows, columns):
    angles = (rows[:, None] * columns[None, :] % N) * (2.0 * math.pi / N)
    return np.cos(angles) + np.sin(angles)


def three_terms(table):
    high = table.astype(np.float32).astype(jnp.bfloat16)
    low = (table - high.astype(np.float64)).astype(np.float32).astype(jnp.bfloat16)
    return np.concatenate([high, high, low], axis=1)


def tables():
    places = np.arange(N)
    return (
        three_terms(cas(places, places)),
        three_terms(cas(FOLD, places)),
        three_terms(cas(places, FOLD)),
    )


def screened_kernel():
    line = jnp.arange(N, dtype=jnp.int32)
    freq = jnp.where(2 * line >= N, line - N, line)
    freq_y = jnp.pad(freq, (0, LANES - N))[None, None, :]
    freq_x = jnp.arange(48, dtype=jnp.int32)[None, :, None]
    freq_z = jnp.concatenate([jnp.arange(HALF + 1), jnp.arange(1, GROUP)]).astype(jnp.int32)[:, None, None]
    squares = (freq_x * freq_x + freq_y * freq_y + freq_z * freq_z).astype(F32)
    wave_square = squares * (2.0 * math.pi / CELL_LENGTH) ** 2
    safe_square = jnp.where(squares == 0, 1.0, wave_square)
    shaped = 4.0 * math.pi / safe_square * (1.0 - jnp.exp(-safe_square / (4.0 * SCREENING**2)))
    kernel = jnp.where(squares == 0, math.pi / SCREENING**2, shaped) * (1.0 / N**3)
    return kernel.reshape(6, GROUP, 48, LANES).transpose(0, 2, 1, 3).reshape(6, 48, GROUP * LANES)


def times(table, data):
    high = data.astype(BF16)
    low = (data - high.astype(F32)).astype(BF16)
    stacked = jnp.concatenate([high, low, high], axis=0)
    return lax.dot_general(table, stacked, (((1,), (0,)), ((), ())), preferred_element_type=F32)


def piece(data, index):
    return data[:, LANES * index : LANES * (index + 1)]


def unit_body(near_a, near_b, far_a, far_b, table_y, table_to, table_from, kernel, total, out, there, back):
    fill = jnp.zeros((LANES - N, LANES), F32)

    def forward(a, b, first, group):
        start = group * PLANES
        density = jnp.concatenate([a[start + i] * b[start + i] for i in range(PLANES)], axis=1)
        along_y = times(table_y[...], density)
        turned = [jnp.concatenate([piece(along_y, i), fill], axis=0).T for i in range(PLANES)]
        rows = [
            jnp.concatenate(
                [turned[j // 2][LOW * (j % 2) : LOW * (j % 2) + LOW], turned[4][HIGH * j : HIGH * (j + 1)]], axis=0
            )
            for j in range(GROUP)
        ]
        along_z = times(table_to[...], jnp.concatenate(rows, axis=1))
        for j in range(GROUP):
            there[first + group * GROUP + j] = piece(along_z, j)

    def middle(group, kernel_group):
        block = there[:, pl.ds(pl.multiple_of(group * GROUP, GROUP), GROUP), :]
        block = jnp.swapaxes(block, 0, 1)
        along_x = times(table_to[...], jnp.concatenate([block[j] for j in range(GROUP)], axis=1))
        values = kernel[kernel_group]
        upper = values[:HALF]
        row = lax.broadcasted_iota(jnp.int32, (8, GROUP * LANES), 0)
        lower = jnp.concatenate(
            [jnp.where(row == 0, values[HALF : HALF + 1], values[:8]), values[8:HALF]], axis=0
        )
        along_x = along_x * jnp.concatenate([upper, lower], axis=0)
        again = times(table_from[:HALF], along_x)
        block = jnp.stack([piece(again, j) for j in range(GROUP)], axis=0)
        back[:, pl.ds(pl.multiple_of(group * GROUP, GROUP), GROUP), :] = jnp.swapaxes(block, 0, 1)

    def backward(group):
        rows = [back[group * GROUP + j] for j in range(GROUP)]
        along_z = times(table_from[...], jnp.concatenate(rows, axis=1))
        parts = [piece(along_z, j) for j in range(GROUP)]
        packed = [jnp.concatenate([parts[2 * i][:LOW], parts[2 * i + 1][:LOW]], axis=0) for i in range(4)]
        packed.append(jnp.concatenate([part[LOW:] for part in parts], axis=0))
        turned = jnp.concatenate([plane.T[:N] for plane in packed], axis=1)
        potential = times(table_y[...], turned)
        start = group * PLANES
        for i in range(PLANES):
            term = piece(potential, i) * near_b[start + i]
            out[start + i] = term if total is None else total[start + i] + term

    @pl.loop(0, GROUPS)
    def _(group):
        forward(near_a, near_b, 0, group)

    @pl.loop(0, GROUPS)
    def _(group):
        forward(far_a, far_b, HALF, group)

    @pl.loop(0, 2 * GROUPS)
    def _(group):
        middle(group, jnp.where(group > GROUPS, group - GROUPS, group))

    @pl.loop(0, GROUPS)
    def _(group):
        backward(group)


def unit(a, b, constants, total=None):
    operands = [a[0], b[0], a[1], b[1], *constants]

    def body(*refs):
        ins, rest = refs[: len(operands)], refs[len(operands) :]
        if total is None:
            unit_body(*ins, None, *rest)
        else:
            unit_body(*ins, *rest)

    return pl.pallas_call(
        body,
        out_shape=jax.ShapeDtypeStruct(PACKED, F32),
        scratch_shapes=[pltpu.VMEM((N, N, LANES), F32), pltpu.VMEM((HALF, N, LANES), F32)],
        compiler_params=pltpu.CompilerParams(vmem_limit_bytes=32 * 2**20),
        cost_estimate=pl.CostEstimate(flops=6 * 10**9, bytes_accessed=8 * 2**20, transcendentals=0),
        name="unit",
    )(*operands, *(() if total is None else (total,)))


def pack_body(data, out):
    lane = lax.broadcasted_iota(jnp.int32, (N, LANES), 1)
    pad = jnp.zeros((N, LANES - N), F32)

    @pl.loop(0, GROUPS)
    def _(group):
        last = None
        for i in range(4):
            pair = [jnp.concatenate([data[group * GROUP + 2 * i + h], pad], axis=1) for h in range(2)]
            out[group * PLANES + i] = jnp.where(lane < LOW, pair[0], pltpu.roll(pair[1], LOW, 1))
            for h in range(2):
                place = HIGH * (2 * i + h)
                moved = pltpu.roll(pair[h], (place - LOW) % LANES, 1) if place != LOW else pair[h]
                last = moved if last is None else jnp.where(lane >= place, moved, last)
        out[group * PLANES + 4] = last


def pack(data):
    return pl.pallas_call(
        pack_body,
        out_shape=jax.ShapeDtypeStruct(PACKED, F32),
        compiler_params=pltpu.CompilerParams(vmem_limit_bytes=16 * 2**20),
        name="pack",
    )(data)


def unpack_body(total, more, out):
    lane = lax.broadcasted_iota(jnp.int32, (N, LANES), 1)

    @pl.loop(0, GROUPS)
    def _(group):
        start = group * PLANES
        planes = [total[start + i] + more[start + i] for i in range(PLANES)]
        for j in range(GROUP):
            low = planes[j // 2] if j % 2 == 0 else pltpu.roll(planes[j // 2], LOW, 1)
            place = HIGH * j
            high = pltpu.roll(planes[4], (LOW - place) % LANES, 1) if place != LOW else planes[4]
            out[group * GROUP + j] = jnp.where(lane < LOW, low, high)[:, :N]


def unpack_sum(total, more):
    return pl.pallas_call(
        unpack_body,
        out_shape=jax.ShapeDtypeStruct((HALF, N, N), F32),
        compiler_params=pltpu.CompilerParams(vmem_limit_bytes=16 * 2**20),
        name="unpack_sum",
    )(total, more)


def shards(orbitals):
    bands = lax.axis_size("band")
    side = [1 if b % 2 else -1 for b in range(bands)]

    def from_place(data, distance):
        route = [((b + distance * side[b]) % bands, b) for b in range(bands)]
        return lax.ppermute(data, "band", route)

    def other_core(data):
        return from_place(data, -1)

    def other_slab(data):
        return lax.ppermute(data, "grid", [(0, 1), (1, 0)])

    constants = tuple(jnp.asarray(t) for t in tables()) + (screened_kernel(),)
    own_near = pack(orbitals[0])
    own_far = other_slab(own_near)
    own = (own_near, own_far)
    m1 = tuple(other_core(d) for d in own)
    m2 = tuple(from_place(d, -2) for d in own)
    p1 = tuple(other_core(d) for d in m2)
    p2 = tuple(from_place(d, 2) for d in own)
    m3 = tuple(other_core(d) for d in p2)
    total = unit(own, m1, constants)
    lent = unit(m2, p1, constants)
    returned = from_place(lent, 2)
    total = unit(own, m2, constants, total)
    total = unit(own, p1, constants, total)
    total = unit(own, p2, constants, total)
    total = unit(own, m3, constants, total)
    return unpack_sum(total, returned)[None]


def solution(mesh):
    spec = P("band", "grid", None, None)
    return jax.shard_map(shards, mesh=mesh, in_specs=(spec,), out_specs=spec, check_vma=False)
```

```python
import functools
import math

import jax
import jax.numpy as jnp
import numpy as np
from jax import lax
from jax.experimental import pallas as pl
from jax.experimental.pallas import tpu as pltpu
from jax.sharding import PartitionSpec as P

CELL_LENGTH = 37.2
SCREENING = 0.106
BF16 = jnp.bfloat16
F32 = jnp.float32
N = 80
HALF = N // 2
GROUP = 8
GROUPS = HALF // GROUP
PLANES = 5
PACKED = (GROUPS * PLANES, N, 128)
LANES = 128
LOW, HIGH = 64, 16

FOLD = np.concatenate([np.arange(HALF), [HALF], np.arange(N - 1, HALF, -1)])


def cas(rows, columns):
    angles = (rows[:, None] * columns[None, :] % N) * (2.0 * math.pi / N)
    return np.cos(angles) + np.sin(angles)


def three_terms(table):
    high = table.astype(np.float32).astype(jnp.bfloat16)
    low = (table - high.astype(np.float64)).astype(np.float32).astype(jnp.bfloat16)
    return np.concatenate([high, high, low], axis=1)


def tables():
    places = np.arange(N)
    return (
        three_terms(cas(places, places)),
        three_terms(cas(FOLD, places)),
        three_terms(cas(places, FOLD)),
    )


def screened_kernel():
    line = jnp.arange(N, dtype=jnp.int32)
    freq = jnp.where(2 * line >= N, line - N, line)
    freq_y = jnp.pad(freq, (0, LANES - N))[None, None, :]
    freq_x = jnp.arange(48, dtype=jnp.int32)[None, :, None]
    freq_z = jnp.concatenate([jnp.arange(HALF + 1), jnp.arange(1, GROUP)]).astype(jnp.int32)[:, None, None]
    squares = (freq_x * freq_x + freq_y * freq_y + freq_z * freq_z).astype(F32)
    wave_square = squares * (2.0 * math.pi / CELL_LENGTH) ** 2
    safe_square = jnp.where(squares == 0, 1.0, wave_square)
    shaped = 4.0 * math.pi / safe_square * (1.0 - jnp.exp(-safe_square / (4.0 * SCREENING**2)))
    kernel = jnp.where(squares == 0, math.pi / SCREENING**2, shaped) * (1.0 / N**3)
    return kernel.reshape(6, GROUP, 48, LANES).transpose(0, 2, 1, 3).reshape(6, 48, GROUP * LANES)


def times(table, data):
    high = data.astype(BF16)
    low = (data - high.astype(F32)).astype(BF16)
    stacked = jnp.concatenate([high, low, high], axis=0)
    return lax.dot_general(table, stacked, (((1,), (0,)), ((), ())), preferred_element_type=F32)


def piece(data, index):
    return data[:, LANES * index : LANES * (index + 1)]


def unit_body(near_a, near_b, far_a, far_b, table_y, table_to, table_from, kernel, total, out, there, back):
    fill = jnp.zeros((LANES - N, LANES), F32)

    def forward(a, b, first, group):
        start = group * PLANES
        density = jnp.concatenate([a[start + i] * b[start + i] for i in range(PLANES)], axis=1)
        along_y = times(table_y[...], density)
        turned = [jnp.concatenate([piece(along_y, i), fill], axis=0).T for i in range(PLANES)]
        rows = [
            jnp.concatenate(
                [turned[j // 2][LOW * (j % 2) : LOW * (j % 2) + LOW], turned[4][HIGH * j : HIGH * (j + 1)]], axis=0
            )
            for j in range(GROUP)
        ]
        along_z = times(table_to[...], jnp.concatenate(rows, axis=1))
        for j in range(GROUP):
            there[first + group * GROUP + j] = piece(along_z, j)

    def middle(group, kernel_group):
        block = there[:, pl.ds(pl.multiple_of(group * GROUP, GROUP), GROUP), :]
        block = jnp.swapaxes(block, 0, 1)
        along_x = times(table_to[...], jnp.concatenate([block[j] for j in range(GROUP)], axis=1))
        values = kernel[kernel_group]
        upper = values[:HALF]
        row = lax.broadcasted_iota(jnp.int32, (8, GROUP * LANES), 0)
        lower = jnp.concatenate(
            [jnp.where(row == 0, values[HALF : HALF + 1], values[:8]), values[8:HALF]], axis=0
        )
        along_x = along_x * jnp.concatenate([upper, lower], axis=0)
        again = times(table_from[:HALF], along_x)
        block = jnp.stack([piece(again, j) for j in range(GROUP)], axis=0)
        back[:, pl.ds(pl.multiple_of(group * GROUP, GROUP), GROUP), :] = jnp.swapaxes(block, 0, 1)

    def backward(group):
        rows = [back[group * GROUP + j] for j in range(GROUP)]
        along_z = times(table_from[...], jnp.concatenate(rows, axis=1))
        parts = [piece(along_z, j) for j in range(GROUP)]
        packed = [jnp.concatenate([parts[2 * i][:LOW], parts[2 * i + 1][:LOW]], axis=0) for i in range(4)]
        packed.append(jnp.concatenate([part[LOW:] for part in parts], axis=0))
        turned = jnp.concatenate([plane.T[:N] for plane in packed], axis=1)
        potential = times(table_y[...], turned)
        start = group * PLANES
        for i in range(PLANES):
            term = piece(potential, i) * near_b[start + i]
            out[start + i] = term if total is None else total[start + i] + term

    for group in range(GROUPS):
        forward(near_a, near_b, 0, group)
        forward(far_a, far_b, HALF, group)
    for group in range(2 * GROUPS):
        middle(group, group - GROUPS if group > GROUPS else group)
    for group in range(GROUPS):
        backward(group)


def unit(a, b, constants, total=None):
    operands = [a[0], b[0], a[1], b[1], *constants]

    def body(*refs):
        ins, rest = refs[: len(operands)], refs[len(operands) :]
        if total is None:
            unit_body(*ins, None, *rest)
        else:
            unit_body(*ins, *rest)

    return pl.pallas_call(
        body,
        out_shape=jax.ShapeDtypeStruct(PACKED, F32),
        scratch_shapes=[pltpu.VMEM((N, N, LANES), F32), pltpu.VMEM((HALF, N, LANES), F32)],
        compiler_params=pltpu.CompilerParams(vmem_limit_bytes=32 * 2**20),
        cost_estimate=pl.CostEstimate(flops=2 * 10**9, bytes_accessed=4 * 2**20, transcendentals=0),
        name="unit",
    )(*operands, *(() if total is None else (total,)))


def pack_body(data, out):
    lane = lax.broadcasted_iota(jnp.int32, (N, LANES), 1)
    pad = jnp.zeros((N, LANES - N), F32)

    @pl.loop(0, GROUPS)
    def _(group):
        last = None
        for i in range(4):
            pair = [jnp.concatenate([data[group * GROUP + 2 * i + h], pad], axis=1) for h in range(2)]
            out[group * PLANES + i] = jnp.where(lane < LOW, pair[0], pltpu.roll(pair[1], LOW, 1))
            for h in range(2):
                place = HIGH * (2 * i + h)
                moved = pltpu.roll(pair[h], (place - LOW) % LANES, 1) if place != LOW else pair[h]
                last = moved if last is None else jnp.where(lane >= place, moved, last)
        out[group * PLANES + 4] = last


def pack(data):
    return pl.pallas_call(
        pack_body,
        out_shape=jax.ShapeDtypeStruct(PACKED, F32),
        compiler_params=pltpu.CompilerParams(vmem_limit_bytes=16 * 2**20),
        name="pack",
    )(data)


def unpack_body(total, more, out):
    lane = lax.broadcasted_iota(jnp.int32, (N, LANES), 1)

    @pl.loop(0, GROUPS)
    def _(group):
        start = group * PLANES
        planes = [total[start + i] + more[start + i] for i in range(PLANES)]
        for j in range(GROUP):
            low = planes[j // 2] if j % 2 == 0 else pltpu.roll(planes[j // 2], LOW, 1)
            place = HIGH * j
            high = pltpu.roll(planes[4], (LOW - place) % LANES, 1) if place != LOW else planes[4]
            out[group * GROUP + j] = jnp.where(lane < LOW, low, high)[:, :N]


def unpack_sum(total, more):
    return pl.pallas_call(
        unpack_body,
        out_shape=jax.ShapeDtypeStruct((HALF, N, N), F32),
        compiler_params=pltpu.CompilerParams(vmem_limit_bytes=16 * 2**20),
        name="unpack_sum",
    )(total, more)


def shards(orbitals):
    bands = lax.axis_size("band")
    half = bands // 2
    place = lax.axis_index("band")
    sides = [1 if b % 2 else -1 for b in range(bands)]

    def sources(distance):
        return [(b + distance * sides[b]) % bands for b in range(bands)]

    def crosses(b, source):
        return b // half != source // half

    def holds(places):
        return functools.reduce(jnp.logical_or, [place == p for p in places])

    def from_place(data, distance):
        return lax.ppermute(data, "band", [(source, b) for b, source in enumerate(sources(distance))])

    def near_inside(data, distance):
        return lax.ppermute(
            data, "band", [(source, b) for b, source in enumerate(sources(distance)) if not crosses(b, source)]
        )

    def near_across(data, inside, distance):
        route = [(source, b) for b, source in enumerate(sources(distance)) if crosses(b, source)]
        across = lax.ppermute(data, "band", route)
        return jnp.where(holds([b for _, b in route]), across, inside)

    def far_route(distance):
        route, across = [], []
        for b, source in enumerate(sources(distance)):
            cross = crosses(b, source)
            if cross:
                across.append(source)
            for slab in range(2):
                route.append((2 * source + (1 - slab if cross else slab), 2 * b + slab))
        return route, holds(across)

    def other_core(data):
        return from_place(data, -1)

    constants = tuple(jnp.asarray(t) for t in tables()) + (screened_kernel(),)
    near = pack(orbitals[0])
    far = lax.ppermute(near, "grid", [(0, 1), (1, 0)])
    m2_inside = near_inside(near, -2)
    p2_inside = near_inside(near, 2)
    near_later, far, m2_inside, p2_inside = lax.optimization_barrier((near, far, m2_inside, p2_inside))
    own = (near, far)
    m2_route, m2_across = far_route(-2)
    p2_route, p2_across = far_route(2)
    m2_sent = jnp.where(m2_across, near, far)
    p2_sent = jnp.where(p2_across, near, far)
    m2_far = lax.ppermute(m2_sent, ("band", "grid"), m2_route)
    m2_near = near_across(near_later, m2_inside, -2)
    m1 = (other_core(near), other_core(far))
    total = unit(own, m1, constants)
    p2_sent, p2_inside, total = lax.optimization_barrier((p2_sent, p2_inside, total))
    p2_far = lax.ppermute(p2_sent, ("band", "grid"), p2_route)
    p2_near = near_across(near_later, p2_inside, 2)
    m2_far, total = lax.optimization_barrier((m2_far, total))
    m2 = (m2_near, m2_far)
    p1 = (other_core(m2_near), other_core(m2_far))
    lent = unit(m2, p1, constants)
    returned = from_place(lent, 2)
    total, lent = lax.optimization_barrier((total, lent))
    total = unit(own, m2, constants, total)
    total = unit(own, p1, constants, total)
    p2_far, total = lax.optimization_barrier((p2_far, total))
    p2 = (p2_near, p2_far)
    m3 = (other_core(p2_near), other_core(p2_far))
    total = unit(own, p2, constants, total)
    total, returned = lax.optimization_barrier((total, returned))
    total = unit(own, m3, constants, total)
    return unpack_sum(total, returned)[None]


def solution(mesh):
    spec = P("band", "grid", None, None)
    return jax.shard_map(shards, mesh=mesh, in_specs=(spec,), out_specs=spec, check_vma=False)
```

```python
import functools
import math

import jax
import jax.numpy as jnp
import numpy as np
from jax import lax
from jax.experimental import pallas as pl
from jax.experimental.pallas import tpu as pltpu
from jax.sharding import PartitionSpec as P

CELL_LENGTH = 37.2
SCREENING = 0.106
BF16 = jnp.bfloat16
F32 = jnp.float32
N = 80
HALF = N // 2
GROUP = 8
GROUPS = HALF // GROUP
PLANES = 5
PACKED = (GROUPS * PLANES, N, 128)
LANES = 128
LOW, HIGH = 64, 16

FOLD = np.concatenate([np.arange(HALF), [HALF], np.arange(N - 1, HALF, -1)])


def cas(rows, columns):
    angles = (rows[:, None] * columns[None, :] % N) * (2.0 * math.pi / N)
    return np.cos(angles) + np.sin(angles)


def three_terms(table):
    high = table.astype(np.float32).astype(jnp.bfloat16)
    low = (table - high.astype(np.float64)).astype(np.float32).astype(jnp.bfloat16)
    return np.concatenate([high, high, low], axis=1)


def tables():
    places = np.arange(N)
    return (
        three_terms(cas(places, places)),
        three_terms(cas(FOLD, places)),
        three_terms(cas(places, FOLD)),
    )


def screened_kernel():
    line = np.arange(N)
    freq_y = np.pad(np.where(2 * line >= N, line - N, line), (0, LANES - N))[None, None, None, :]
    freq_x = np.arange(HALF + 1)[None, :, None, None]
    freq_z = np.concatenate([np.arange(HALF + 1), np.arange(1, GROUP)]).reshape(6, 1, GROUP, 1)
    squares = freq_x * freq_x + freq_y * freq_y + freq_z * freq_z
    wave_square = np.where(squares == 0, 1, squares) * (2.0 * math.pi / CELL_LENGTH) ** 2
    shaped = 4.0 * math.pi / wave_square * (1.0 - np.exp(-wave_square / (4.0 * SCREENING**2)))
    return (np.where(squares == 0, math.pi / SCREENING**2, shaped) * (1.0 / N**3)).astype(np.float32)


def point(n1, n2):
    return (5 * n1 + 16 * n2) % N


def frequency(k1, k2):
    k = next(k for k in range(N) if k % 16 == k1 and k % 5 == k2)
    return min(k, N - k)


def turn(re, im, k, n, sign):
    if k == 0:
        return re, im
    if 4 * k == n:
        return (-im, re) if sign > 0 else (im, -re)
    c, s = math.cos(2 * math.pi * k / n), sign * math.sin(2 * math.pi * k / n)
    if 8 * k == n:
        return c * (re - sign * im), c * (im + sign * re)
    if 8 * k == 3 * n:
        return c * (re + sign * im), c * (im - sign * re)
    return c * re - s * im, c * im + s * re


def real_transform(x):
    n = len(x)
    if n == 2:
        return [(x[0] + x[1], None), (x[0] - x[1], None)]
    even, odd = real_transform(x[0::2]), real_transform(x[1::2])
    out = [None] * (n // 2 + 1)
    out[0] = (even[0][0] + odd[0][0], None)
    out[n // 2] = (even[0][0] - odd[0][0], None)
    out[n // 4] = (even[n // 4][0], -odd[n // 4][0])
    for k in range(1, n // 4):
        re, im = turn(*odd[k], k, n, -1)
        out[k] = (even[k][0] + re, even[k][1] + im)
        out[n // 2 - k] = (even[k][0] - re, im - even[k][1])
    return out


def real_inverse(spectrum):
    n = 2 * (len(spectrum) - 1)
    if n == 2:
        return [spectrum[0][0] + spectrum[1][0], spectrum[0][0] - spectrum[1][0]]
    even, odd = [None] * (n // 4 + 1), [None] * (n // 4 + 1)
    even[0] = (spectrum[0][0] + spectrum[n // 2][0], None)
    odd[0] = (spectrum[0][0] - spectrum[n // 2][0], None)
    even[n // 4] = (2.0 * spectrum[n // 4][0], None)
    odd[n // 4] = (-2.0 * spectrum[n // 4][1], None)
    for k in range(1, n // 4):
        (re, im), (re_far, im_far) = spectrum[k], spectrum[n // 2 - k]
        even[k] = (re + re_far, im - im_far)
        odd[k] = turn(re - re_far, im + im_far, k, n, 1)
    out = [None] * n
    out[0::2], out[1::2] = real_inverse(even), real_inverse(odd)
    return out


C1, C2 = math.cos(2 * math.pi / 5), math.cos(4 * math.pi / 5)
S1, S2 = math.sin(2 * math.pi / 5), math.sin(4 * math.pi / 5)


def five_parts(x):
    t1, t2, t3, t4 = x[1] + x[4], x[2] + x[3], x[1] - x[4], x[2] - x[3]
    return (
        x[0] + t1 + t2,
        x[0] + C1 * t1 + C2 * t2,
        x[0] + C2 * t1 + C1 * t2,
        S1 * t3 + S2 * t4,
        S2 * t3 - S1 * t4,
    )


def five_real(x, kernel):
    zero, a1, a2, b1, b2 = five_parts(x)
    zero, a1, a2, b1, b2 = kernel[0] * zero, 2.0 * kernel[1] * a1, 2.0 * kernel[2] * a2, 2.0 * kernel[1] * b1, 2.0 * kernel[2] * b2
    m1, m2 = zero + C1 * a1 + C2 * a2, zero + C2 * a1 + C1 * a2
    n1, n2 = S1 * b1 + S2 * b2, S2 * b1 - S1 * b2
    return [zero + a1 + a2, m1 + n1, m2 + n2, m2 - n2, m1 - n1]


def five_complex(re, im, kernel):
    r0, ra1, ra2, rb1, rb2 = five_parts(re)
    i0, ia1, ia2, ib1, ib2 = five_parts(im)
    r = [kernel[0] * r0, kernel[1] * (ra1 + ib1), kernel[2] * (ra2 + ib2), kernel[3] * (ra2 - ib2), kernel[4] * (ra1 - ib1)]
    i = [kernel[0] * i0, kernel[1] * (ia1 - rb1), kernel[2] * (ia2 - rb2), kernel[3] * (ia2 + rb2), kernel[4] * (ia1 + rb1)]
    r0, ra1, ra2, rb1, rb2 = five_parts(r)
    i0, ia1, ia2, ib1, ib2 = five_parts(i)
    return (
        [r0, ra1 - ib1, ra2 - ib2, ra2 + ib2, ra1 + ib1],
        [i0, ia1 + rb1, ia2 + rb2, ia2 - rb2, ia1 - rb1],
    )


def times(table, data):
    high = data.astype(BF16)
    low = (data - high.astype(F32)).astype(BF16)
    stacked = jnp.concatenate([high, low, high], axis=0)
    return lax.dot_general(table, stacked, (((1,), (0,)), ((), ())), preferred_element_type=F32)


def piece(data, index):
    return data[:, LANES * index : LANES * (index + 1)]


def unit_body(near_a, near_b, far_a, far_b, table_y, table_to, table_from, kernel, total, out, there, back, mid, turned):
    fill = jnp.zeros((LANES - N, LANES), F32)

    def forward_y(a, b, first, group):
        start = group * PLANES
        density = jnp.concatenate([a[start + i] * b[start + i] for i in range(PLANES)], axis=1)
        along_y = times(table_y[...], density)
        for i in range(PLANES):
            turned[first + start + i] = jnp.concatenate([piece(along_y, i), fill], axis=0).T

    def forward_z(group):
        start = group * PLANES
        rows = [
            jnp.concatenate(
                [
                    turned[start + j // 2, LOW * (j % 2) : LOW * (j % 2) + LOW],
                    turned[start + 4, HIGH * j : HIGH * (j + 1)],
                ],
                axis=0,
            )
            for j in range(GROUP)
        ]
        along_z = times(table_to[...], jnp.concatenate(rows, axis=1))
        for j in range(GROUP):
            there[group * GROUP + j] = piece(along_z, j)

    def middle(group, kernel_group):
        rows = pl.ds(pl.multiple_of(group * GROUP, GROUP), GROUP)
        for n2 in range(5):
            for k1, (re, im) in enumerate(real_transform([there[point(n1, n2), rows, :] for n1 in range(16)])):
                mid[2 * k1, n2] = re
                if im is not None:
                    mid[2 * k1 + 1, n2] = im
        for k1 in range(9):
            scale = [kernel[kernel_group, frequency(k1, k2)] for k2 in range(5)]
            re = [mid[2 * k1, n2] for n2 in range(5)]
            if k1 in (0, 8):
                re = five_real(re, scale)
            else:
                re, im = five_complex(re, [mid[2 * k1 + 1, n2] for n2 in range(5)], scale)
                for n2 in range(5):
                    mid[2 * k1 + 1, n2] = im[n2]
            for n2 in range(5):
                mid[2 * k1, n2] = re[n2]
        for n2 in range(5):
            spectrum = [(mid[2 * k1, n2], None if k1 in (0, 8) else mid[2 * k1 + 1, n2]) for k1 in range(9)]
            for n1, value in enumerate(real_inverse(spectrum)):
                if point(n1, n2) < HALF:
                    back[point(n1, n2), rows, :] = value

    def backward_z(group):
        rows = [back[group * GROUP + j] for j in range(GROUP)]
        along_z = times(table_from[...], jnp.concatenate(rows, axis=1))
        parts = [piece(along_z, j) for j in range(GROUP)]
        packed = [jnp.concatenate([parts[2 * i][:LOW], parts[2 * i + 1][:LOW]], axis=0) for i in range(4)]
        packed.append(jnp.concatenate([part[LOW:] for part in parts], axis=0))
        for i, plane in enumerate(packed):
            turned[group * PLANES + i] = plane.T

    def backward_y(group):
        start = group * PLANES
        planes = jnp.concatenate([turned[start + i, :N] for i in range(PLANES)], axis=1)
        potential = times(table_y[...], planes)
        for i in range(PLANES):
            term = piece(potential, i) * near_b[start + i]
            out[start + i] = term if total is None else total[start + i] + term

    for group in range(GROUPS):
        forward_y(near_a, near_b, 0, group)
        forward_y(far_a, far_b, GROUPS * PLANES, group)
    for group in range(2 * GROUPS):
        forward_z(group)

    @pl.loop(0, 2 * GROUPS)
    def _(group):
        middle(group, jnp.where(group > GROUPS, group - GROUPS, group))

    for group in range(GROUPS):
        backward_z(group)
    for group in range(GROUPS):
        backward_y(group)


def unit(a, b, constants, total=None):
    operands = [a[0], b[0], a[1], b[1], *constants]

    def body(*refs):
        ins, rest = refs[: len(operands)], refs[len(operands) :]
        if total is None:
            unit_body(*ins, None, *rest)
        else:
            unit_body(*ins, *rest)

    return pl.pallas_call(
        body,
        out_shape=jax.ShapeDtypeStruct(PACKED, F32),
        scratch_shapes=[pltpu.VMEM((N, N, LANES), F32), pltpu.VMEM((HALF, N, LANES), F32), pltpu.VMEM((17, 5, GROUP, LANES), F32), pltpu.VMEM((2 * GROUPS * PLANES, LANES, LANES), F32)],
        compiler_params=pltpu.CompilerParams(vmem_limit_bytes=20 * 2**20),
        cost_estimate=pl.CostEstimate(flops=10**9, bytes_accessed=2**20, transcendentals=0),
        name="unit",
    )(*operands, *(() if total is None else (total,)))


def pack_body(data, out):
    lane = lax.broadcasted_iota(jnp.int32, (N, LANES), 1)
    pad = jnp.zeros((N, LANES - N), F32)

    @pl.loop(0, GROUPS)
    def _(group):
        last = None
        for i in range(4):
            pair = [jnp.concatenate([data[group * GROUP + 2 * i + h], pad], axis=1) for h in range(2)]
            out[group * PLANES + i] = jnp.where(lane < LOW, pair[0], pltpu.roll(pair[1], LOW, 1))
            for h in range(2):
                place = HIGH * (2 * i + h)
                moved = pltpu.roll(pair[h], (place - LOW) % LANES, 1) if place != LOW else pair[h]
                last = moved if last is None else jnp.where(lane >= place, moved, last)
        out[group * PLANES + 4] = last


def pack(data):
    return pl.pallas_call(
        pack_body,
        out_shape=jax.ShapeDtypeStruct(PACKED, F32),
        compiler_params=pltpu.CompilerParams(vmem_limit_bytes=16 * 2**20),
        name="pack",
    )(data)


def unpack_body(total, returned, theirs, out):
    lane = lax.broadcasted_iota(jnp.int32, (N, LANES), 1)

    @pl.loop(0, GROUPS)
    def _(group):
        start = group * PLANES
        planes = [total[start + i] + returned[start + i] + theirs[start + i] for i in range(PLANES)]
        for j in range(GROUP):
            low = planes[j // 2] if j % 2 == 0 else pltpu.roll(planes[j // 2], LOW, 1)
            place = HIGH * j
            high = pltpu.roll(planes[4], (LOW - place) % LANES, 1) if place != LOW else planes[4]
            out[group * GROUP + j] = jnp.where(lane < LOW, low, high)[:, :N]


def unpack_sum(total, returned, theirs):
    return pl.pallas_call(
        unpack_body,
        out_shape=jax.ShapeDtypeStruct((HALF, N, N), F32),
        compiler_params=pltpu.CompilerParams(vmem_limit_bytes=16 * 2**20),
        name="unpack_sum",
    )(total, returned, theirs)


def shards(orbitals):
    bands = lax.axis_size("band")
    half = bands // 2
    place = lax.axis_index("band")
    sides = [1 if b % 2 else -1 for b in range(bands)]

    def sources(distance):
        return [(b + distance * sides[b]) % bands for b in range(bands)]

    def crosses(b, source):
        return b // half != source // half

    def holds(places):
        return functools.reduce(jnp.logical_or, [place == p for p in places])

    def from_place(data, distance):
        return lax.ppermute(data, "band", [(source, b) for b, source in enumerate(sources(distance))])

    def near_inside(data, distance):
        return lax.ppermute(
            data, "band", [(source, b) for b, source in enumerate(sources(distance)) if not crosses(b, source)]
        )

    def near_across(data, distance):
        route = [(source, b) for b, source in enumerate(sources(distance)) if crosses(b, source)]
        return lax.ppermute(data, "band", route), holds([b for _, b in route])

    def far_route(distance):
        route, across = [], []
        for b, source in enumerate(sources(distance)):
            cross = crosses(b, source)
            if cross:
                across.append(source)
            for slab in range(2):
                route.append((2 * source + (1 - slab if cross else slab), 2 * b + slab))
        return route, holds(across)

    def other_core(data):
        return from_place(data, -1)

    constants = tuple(jnp.asarray(t) for t in (*tables(), screened_kernel()))
    near = pack(orbitals[0])
    far = lax.ppermute(near, "grid", [(0, 1), (1, 0)])
    m2_inside = near_inside(near, -2)
    p2_inside = near_inside(near, 2)
    near_later, far, m2_inside, p2_inside = lax.optimization_barrier((near, far, m2_inside, p2_inside))
    own = (near, far)
    m2_route, m2_across = far_route(-2)
    p2_route, p2_across = far_route(2)
    m2_sent = jnp.where(m2_across, near, far)
    p2_sent = jnp.where(p2_across, near, far)
    m2_far = lax.ppermute(m2_sent, ("band", "grid"), m2_route)
    m2_crossed, m2_takes = near_across(near_later, -2)
    m1 = (other_core(near), other_core(far))
    total = unit(own, m1, constants)
    p2_sent, m2_inside, total = lax.optimization_barrier((p2_sent, m2_inside, total))
    p2_far = lax.ppermute(p2_sent, ("band", "grid"), p2_route)
    p2_crossed, p2_takes = near_across(near_later, 2)
    m2_near = jnp.where(m2_takes, m2_crossed, m2_inside)
    p1_near = other_core(m2_near)
    m2_far, p1_near, total = lax.optimization_barrier((m2_far, p1_near, total))
    m2 = (m2_near, m2_far)
    p1_far = other_core(m2_far)
    total = unit(own, m2, constants, total)
    p1_near, total = lax.optimization_barrier((p1_near, total))
    lent = unit(m2, (p1_near, p1_far), constants)
    returned = from_place(lent, 2)
    m2_near, lent = lax.optimization_barrier((m2_near, lent))
    partner = unit(m1, (m2_near, m2_far), constants)
    p2_far, p2_inside, partner, total = lax.optimization_barrier((p2_far, p2_inside, partner, total))
    p2 = (jnp.where(p2_takes, p2_crossed, p2_inside), p2_far)
    partner = unit(m1, p2, constants, partner)
    theirs = other_core(partner)
    total, partner = lax.optimization_barrier((total, partner))
    total = unit(own, p2, constants, total)
    return unpack_sum(total, returned, theirs)[None]


def solution(mesh):
    spec = P("band", "grid", None, None)
    return jax.shard_map(shards, mesh=mesh, in_specs=(spec,), out_specs=spec, check_vma=False)
```

```python
import functools
import math

import jax
import jax.numpy as jnp
import numpy as np
from jax import lax
from jax.experimental import pallas as pl
from jax.experimental.pallas import tpu as pltpu
from jax.sharding import PartitionSpec as P

CELL_LENGTH = 37.2
SCREENING = 0.106
BF16 = jnp.bfloat16
F32 = jnp.float32
N = 80
HALF = N // 2
GROUP = 8
GROUPS = HALF // GROUP
PLANES = 5
PACKED = (GROUPS * PLANES, N, 128)
LANES = 128
LOW, HIGH = 64, 16

FOLD = np.concatenate([np.arange(HALF), [HALF], np.arange(N - 1, HALF, -1)])


def cas(rows, columns):
    angles = (rows[:, None] * columns[None, :] % N) * (2.0 * math.pi / N)
    return np.cos(angles) + np.sin(angles)


def three_terms(table):
    high = table.astype(np.float32).astype(jnp.bfloat16)
    low = (table - high.astype(np.float64)).astype(np.float32).astype(jnp.bfloat16)
    return np.concatenate([high, high, low], axis=1)


def tables():
    places = np.arange(N)
    return (
        three_terms(cas(places, places)),
        three_terms(cas(FOLD, places)),
        three_terms(cas(places, FOLD)),
    )


def screened_kernel():
    line = np.arange(N)
    freq_y = np.pad(np.where(2 * line >= N, line - N, line), (0, LANES - N))[None, None, None, :]
    freq_x = np.arange(HALF + 1)[None, :, None, None]
    freq_z = np.concatenate([np.arange(HALF + 1), np.arange(1, GROUP)]).reshape(6, 1, GROUP, 1)
    squares = freq_x * freq_x + freq_y * freq_y + freq_z * freq_z
    wave_square = np.where(squares == 0, 1, squares) * (2.0 * math.pi / CELL_LENGTH) ** 2
    shaped = 4.0 * math.pi / wave_square * (1.0 - np.exp(-wave_square / (4.0 * SCREENING**2)))
    return (np.where(squares == 0, math.pi / SCREENING**2, shaped) * (1.0 / N**3)).astype(np.float32)


def point(n1, n2):
    return (5 * n1 + 16 * n2) % N


def frequency(k1, k2):
    k = next(k for k in range(N) if k % 16 == k1 and k % 5 == k2)
    return min(k, N - k)


def turn(re, im, k, n, sign):
    if k == 0:
        return re, im
    if 4 * k == n:
        return (-im, re) if sign > 0 else (im, -re)
    c, s = math.cos(2 * math.pi * k / n), sign * math.sin(2 * math.pi * k / n)
    if 8 * k == n:
        return c * (re - sign * im), c * (im + sign * re)
    if 8 * k == 3 * n:
        return c * (re + sign * im), c * (im - sign * re)
    return c * re - s * im, c * im + s * re


def real_transform(x):
    n = len(x)
    if n == 2:
        return [(x[0] + x[1], None), (x[0] - x[1], None)]
    even, odd = real_transform(x[0::2]), real_transform(x[1::2])
    out = [None] * (n // 2 + 1)
    out[0] = (even[0][0] + odd[0][0], None)
    out[n // 2] = (even[0][0] - odd[0][0], None)
    out[n // 4] = (even[n // 4][0], -odd[n // 4][0])
    for k in range(1, n // 4):
        re, im = turn(*odd[k], k, n, -1)
        out[k] = (even[k][0] + re, even[k][1] + im)
        out[n // 2 - k] = (even[k][0] - re, im - even[k][1])
    return out


def real_inverse(spectrum):
    n = 2 * (len(spectrum) - 1)
    if n == 2:
        return [spectrum[0][0] + spectrum[1][0], spectrum[0][0] - spectrum[1][0]]
    even, odd = [None] * (n // 4 + 1), [None] * (n // 4 + 1)
    even[0] = (spectrum[0][0] + spectrum[n // 2][0], None)
    odd[0] = (spectrum[0][0] - spectrum[n // 2][0], None)
    even[n // 4] = (2.0 * spectrum[n // 4][0], None)
    odd[n // 4] = (-2.0 * spectrum[n // 4][1], None)
    for k in range(1, n // 4):
        (re, im), (re_far, im_far) = spectrum[k], spectrum[n // 2 - k]
        even[k] = (re + re_far, im - im_far)
        odd[k] = turn(re - re_far, im + im_far, k, n, 1)
    out = [None] * n
    out[0::2], out[1::2] = real_inverse(even), real_inverse(odd)
    return out


C1, C2 = math.cos(2 * math.pi / 5), math.cos(4 * math.pi / 5)
S1, S2 = math.sin(2 * math.pi / 5), math.sin(4 * math.pi / 5)


def five_parts(x):
    t1, t2, t3, t4 = x[1] + x[4], x[2] + x[3], x[1] - x[4], x[2] - x[3]
    return (
        x[0] + t1 + t2,
        x[0] + C1 * t1 + C2 * t2,
        x[0] + C2 * t1 + C1 * t2,
        S1 * t3 + S2 * t4,
        S2 * t3 - S1 * t4,
    )


def five_real(x, kernel):
    zero, a1, a2, b1, b2 = five_parts(x)
    zero, a1, a2, b1, b2 = kernel[0] * zero, 2.0 * kernel[1] * a1, 2.0 * kernel[2] * a2, 2.0 * kernel[1] * b1, 2.0 * kernel[2] * b2
    m1, m2 = zero + C1 * a1 + C2 * a2, zero + C2 * a1 + C1 * a2
    n1, n2 = S1 * b1 + S2 * b2, S2 * b1 - S1 * b2
    return [zero + a1 + a2, m1 + n1, m2 + n2, m2 - n2, m1 - n1]


def five_complex(re, im, kernel):
    r0, ra1, ra2, rb1, rb2 = five_parts(re)
    i0, ia1, ia2, ib1, ib2 = five_parts(im)
    r = [kernel[0] * r0, kernel[1] * (ra1 + ib1), kernel[2] * (ra2 + ib2), kernel[3] * (ra2 - ib2), kernel[4] * (ra1 - ib1)]
    i = [kernel[0] * i0, kernel[1] * (ia1 - rb1), kernel[2] * (ia2 - rb2), kernel[3] * (ia2 + rb2), kernel[4] * (ia1 + rb1)]
    r0, ra1, ra2, rb1, rb2 = five_parts(r)
    i0, ia1, ia2, ib1, ib2 = five_parts(i)
    return (
        [r0, ra1 - ib1, ra2 - ib2, ra2 + ib2, ra1 + ib1],
        [i0, ia1 + rb1, ia2 + rb2, ia2 - rb2, ia1 - rb1],
    )


def times(table, data):
    high = data.astype(BF16)
    low = (data - high.astype(F32)).astype(BF16)
    stacked = jnp.concatenate([high, low, high], axis=0)
    return lax.dot_general(table, stacked, (((1,), (0,)), ((), ())), preferred_element_type=F32)


def piece(data, index):
    return data[:, LANES * index : LANES * (index + 1)]


def unit_body(near_a, near_b, far_a, far_b, table_y, table_to, table_from, kernel, total, out, done, there, back, mid, turned):
    done[0, 0] = 0
    fill = jnp.zeros((LANES - N, LANES), F32)

    def forward_y(a, b, first, group):
        start = group * PLANES
        density = jnp.concatenate([a[start + i] * b[start + i] for i in range(PLANES)], axis=1)
        along_y = times(table_y[...], density)
        for i in range(PLANES):
            turned[first + start + i] = jnp.concatenate([piece(along_y, i), fill], axis=0).T

    def forward_z(group):
        start = group * PLANES
        rows = [
            jnp.concatenate(
                [
                    turned[start + j // 2, LOW * (j % 2) : LOW * (j % 2) + LOW],
                    turned[start + 4, HIGH * j : HIGH * (j + 1)],
                ],
                axis=0,
            )
            for j in range(GROUP)
        ]
        along_z = times(table_to[...], jnp.concatenate(rows, axis=1))
        for j in range(GROUP):
            there[group * GROUP + j] = piece(along_z, j)

    def middle(group, kernel_group):
        rows = pl.ds(pl.multiple_of(group * GROUP, GROUP), GROUP)
        for n2 in range(5):
            for k1, (re, im) in enumerate(real_transform([there[point(n1, n2), rows, :] for n1 in range(16)])):
                mid[2 * k1, n2] = re
                if im is not None:
                    mid[2 * k1 + 1, n2] = im
        for k1 in range(9):
            scale = [kernel[kernel_group, frequency(k1, k2)] for k2 in range(5)]
            re = [mid[2 * k1, n2] for n2 in range(5)]
            if k1 in (0, 8):
                re = five_real(re, scale)
            else:
                re, im = five_complex(re, [mid[2 * k1 + 1, n2] for n2 in range(5)], scale)
                for n2 in range(5):
                    mid[2 * k1 + 1, n2] = im[n2]
            for n2 in range(5):
                mid[2 * k1, n2] = re[n2]
        for n2 in range(5):
            spectrum = [(mid[2 * k1, n2], None if k1 in (0, 8) else mid[2 * k1 + 1, n2]) for k1 in range(9)]
            for n1, value in enumerate(real_inverse(spectrum)):
                if point(n1, n2) < HALF:
                    back[point(n1, n2), rows, :] = value

    def backward_z(group):
        rows = [back[group * GROUP + j] for j in range(GROUP)]
        along_z = times(table_from[...], jnp.concatenate(rows, axis=1))
        parts = [piece(along_z, j) for j in range(GROUP)]
        packed = [jnp.concatenate([parts[2 * i][:LOW], parts[2 * i + 1][:LOW]], axis=0) for i in range(4)]
        packed.append(jnp.concatenate([part[LOW:] for part in parts], axis=0))
        for i, plane in enumerate(packed):
            turned[group * PLANES + i] = plane.T

    def backward_y(group):
        start = group * PLANES
        planes = jnp.concatenate([turned[start + i, :N] for i in range(PLANES)], axis=1)
        potential = times(table_y[...], planes)
        for i in range(PLANES):
            term = piece(potential, i) * near_b[start + i]
            out[start + i] = term if total is None else total[start + i] + term

    for group in range(GROUPS):
        forward_y(near_a, near_b, 0, group)
        forward_y(far_a, far_b, GROUPS * PLANES, group)
    for group in range(2 * GROUPS):
        forward_z(group)

    @pl.loop(0, 2 * GROUPS)
    def _(group):
        middle(group, jnp.where(group > GROUPS, group - GROUPS, group))

    for group in range(GROUPS):
        backward_z(group)
    for group in range(GROUPS):
        backward_y(group)


def unit(a, b, constants, after, total=None, waits=()):
    operands = [a[0], b[0], a[1], b[1], *constants]

    def body(order, *refs):
        refs = refs[len(waits) :]
        ins, rest = refs[: len(operands)], refs[len(operands) :]
        if total is None:
            unit_body(*ins, None, *rest)
        else:
            unit_body(*ins, *rest)

    here = pl.BlockSpec(memory_space=pltpu.VMEM)
    scalar = pl.BlockSpec(memory_space=pltpu.SMEM)
    operands_all = (*operands, *(() if total is None else (total,)))
    return pl.pallas_call(
        body,
        in_specs=[scalar] + [pl.BlockSpec(memory_space=pl.ANY)] * len(waits) + [here] * len(operands_all),
        out_specs=(here, scalar),
        out_shape=(jax.ShapeDtypeStruct(PACKED, F32), jax.ShapeDtypeStruct((1, 1), jnp.int32)),
        scratch_shapes=[
            pltpu.VMEM((N, N, LANES), F32),
            pltpu.VMEM((HALF, N, LANES), F32),
            pltpu.VMEM((17, 5, GROUP, LANES), F32),
            pltpu.VMEM((2 * GROUPS * PLANES, LANES, LANES), F32),
        ],
        compiler_params=pltpu.CompilerParams(vmem_limit_bytes=20 * 2**20),
        cost_estimate=pl.CostEstimate(flops=1, bytes_accessed=1, transcendentals=0),
        name="unit",
    )(after, *waits, *operands_all)


def choose_body(order, flag, a, b, out):
    @pl.loop(0, GROUPS * PLANES)
    def _(plane):
        out[plane] = jnp.where(flag[0, 0] != 0, a[plane], b[plane])


def choose(flag, a, b, after):
    here = pl.BlockSpec(memory_space=pltpu.VMEM)
    scalar = pl.BlockSpec(memory_space=pltpu.SMEM)
    return pl.pallas_call(
        choose_body,
        in_specs=[scalar, scalar, here, here],
        out_specs=here,
        out_shape=jax.ShapeDtypeStruct(PACKED, F32),
        compiler_params=pltpu.CompilerParams(vmem_limit_bytes=8 * 2**20),
        cost_estimate=pl.CostEstimate(flops=1, bytes_accessed=1, transcendentals=0),
        name="choose",
    )(after, flag.astype(jnp.int32).reshape(1, 1), a, b)


def pack_body(data, out):
    lane = lax.broadcasted_iota(jnp.int32, (N, LANES), 1)
    pad = jnp.zeros((N, LANES - N), F32)

    @pl.loop(0, GROUPS)
    def _(group):
        last = None
        for i in range(4):
            pair = [jnp.concatenate([data[group * GROUP + 2 * i + h], pad], axis=1) for h in range(2)]
            out[group * PLANES + i] = jnp.where(lane < LOW, pair[0], pltpu.roll(pair[1], LOW, 1))
            for h in range(2):
                place = HIGH * (2 * i + h)
                moved = pltpu.roll(pair[h], (place - LOW) % LANES, 1) if place != LOW else pair[h]
                last = moved if last is None else jnp.where(lane >= place, moved, last)
        out[group * PLANES + 4] = last


def pack(data):
    return pl.pallas_call(
        pack_body,
        out_shape=jax.ShapeDtypeStruct(PACKED, F32),
        compiler_params=pltpu.CompilerParams(vmem_limit_bytes=16 * 2**20),
        name="pack",
    )(data)


def unpack_body(total, returned, theirs, out):
    lane = lax.broadcasted_iota(jnp.int32, (N, LANES), 1)

    @pl.loop(0, GROUPS)
    def _(group):
        start = group * PLANES
        planes = [total[start + i] + returned[start + i] + theirs[start + i] for i in range(PLANES)]
        for j in range(GROUP):
            low = planes[j // 2] if j % 2 == 0 else pltpu.roll(planes[j // 2], LOW, 1)
            place = HIGH * j
            high = pltpu.roll(planes[4], (LOW - place) % LANES, 1) if place != LOW else planes[4]
            out[group * GROUP + j] = jnp.where(lane < LOW, low, high)[:, :N]


def unpack_sum(total, returned, theirs):
    return pl.pallas_call(
        unpack_body,
        out_shape=jax.ShapeDtypeStruct((HALF, N, N), F32),
        compiler_params=pltpu.CompilerParams(vmem_limit_bytes=16 * 2**20),
        name="unpack_sum",
    )(total, returned, theirs)


def shards(orbitals):
    bands = lax.axis_size("band")
    half = bands // 2
    place = lax.axis_index("band")
    sides = [1 if b % 2 else -1 for b in range(bands)]

    def sources(distance):
        return [(b + distance * sides[b]) % bands for b in range(bands)]

    def crosses(b, source):
        return b // half != source // half

    def holds(places):
        return functools.reduce(jnp.logical_or, [place == p for p in places])

    def from_place(data, distance):
        return lax.ppermute(data, "band", [(source, b) for b, source in enumerate(sources(distance))])

    def near_inside(data, distance):
        return lax.ppermute(
            data, "band", [(source, b) for b, source in enumerate(sources(distance)) if not crosses(b, source)]
        )

    def near_across(data, distance):
        route = [(source, b) for b, source in enumerate(sources(distance)) if crosses(b, source)]
        return lax.ppermute(data, "band", route), holds([b for _, b in route])

    def far_route(distance):
        route, across = [], []
        for b, source in enumerate(sources(distance)):
            cross = crosses(b, source)
            if cross:
                across.append(source)
            for slab in range(2):
                route.append((2 * source + (1 - slab if cross else slab), 2 * b + slab))
        return route, holds(across)

    def other_core(data):
        return from_place(data, -1)

    constants = tuple(jnp.asarray(t) for t in (*tables(), screened_kernel()))
    near = pack(orbitals[0])
    far = lax.ppermute(near, "grid", [(0, 1), (1, 0)])
    m2_inside = near_inside(near, -2)
    p2_inside = near_inside(near, 2)
    near_later, far = lax.optimization_barrier((near, far))
    own = (near, far)
    m2_route, m2_across = far_route(-2)
    p2_route, p2_across = far_route(2)
    first = jnp.zeros((1, 1), jnp.int32)
    m2_far = lax.ppermute(choose(m2_across, near, far, first), ("band", "grid"), m2_route)
    m2_crossed, m2_takes = near_across(near_later, -2)
    p2_crossed, p2_takes = near_across(near_later, 2)
    m1 = (other_core(near), other_core(far))
    total, after = unit(own, m1, constants, first, waits=(m2_inside, p2_inside))
    p2_far = lax.ppermute(choose(p2_across, near, far, after), ("band", "grid"), p2_route)
    m2 = (choose(m2_takes, m2_crossed, m2_inside, after), m2_far)
    p1 = (other_core(m2[0]), other_core(m2_far))
    total, after = unit(own, m2, constants, after, total)
    lent, after = unit(m2, p1, constants, after)
    returned = from_place(lent, 2)
    partner, after = unit(m1, m2, constants, after, waits=(p2_far,))
    p2 = (choose(p2_takes, p2_crossed, p2_inside, after), p2_far)
    partner, after = unit(m1, p2, constants, after, partner)
    theirs = other_core(partner)
    total, after = unit(own, p2, constants, after, total, waits=(returned,))
    return unpack_sum(total, returned, theirs)[None]


def solution(mesh):
    spec = P("band", "grid", None, None)
    return jax.shard_map(shards, mesh=mesh, in_specs=(spec,), out_specs=spec, check_vma=False)
```

```python
import functools
import math

import jax
import jax.numpy as jnp
import numpy as np
from jax import lax
from jax.experimental import pallas as pl
from jax.experimental.pallas import tpu as pltpu
from jax.sharding import PartitionSpec as P

CELL_LENGTH = 37.2
SCREENING = 0.106
BF16 = jnp.bfloat16
F32 = jnp.float32
N = 80
HALF = N // 2
GROUP = 8
GROUPS = HALF // GROUP
PLANES = 5
PACKED = (GROUPS * PLANES, N, 128)
LANES = 128
LOW, HIGH = 64, 16

FOLD = np.concatenate([np.arange(HALF), [HALF], np.arange(N - 1, HALF, -1)])


def cas(rows, columns):
    angles = (rows[:, None] * columns[None, :] % N) * (2.0 * math.pi / N)
    return np.cos(angles) + np.sin(angles)


def three_terms(table):
    high = table.astype(np.float32).astype(jnp.bfloat16)
    low = (table - high.astype(np.float64)).astype(np.float32).astype(jnp.bfloat16)
    return np.concatenate([high, high, low], axis=1)


def tables():
    places = np.arange(N)
    return (
        three_terms(cas(places, places)),
        three_terms(cas(FOLD, places)),
        three_terms(cas(places, FOLD)),
    )


def screened_kernel():
    line = np.arange(N)
    freq_y = np.pad(np.where(2 * line >= N, line - N, line), (0, LANES - N))[None, None, None, :]
    freq_x = np.arange(HALF + 1)[None, :, None, None]
    freq_z = np.concatenate([np.arange(HALF + 1), np.arange(1, GROUP)]).reshape(6, 1, GROUP, 1)
    squares = freq_x * freq_x + freq_y * freq_y + freq_z * freq_z
    wave_square = np.where(squares == 0, 1, squares) * (2.0 * math.pi / CELL_LENGTH) ** 2
    shaped = 4.0 * math.pi / wave_square * (1.0 - np.exp(-wave_square / (4.0 * SCREENING**2)))
    return (np.where(squares == 0, math.pi / SCREENING**2, shaped) * (1.0 / N**3)).astype(np.float32)


def point(n1, n2):
    return (5 * n1 + 16 * n2) % N


def frequency(k1, k2):
    k = next(k for k in range(N) if k % 16 == k1 and k % 5 == k2)
    return min(k, N - k)


def turn(re, im, k, n, sign):
    if k == 0:
        return re, im
    if 4 * k == n:
        return (-im, re) if sign > 0 else (im, -re)
    c, s = math.cos(2 * math.pi * k / n), sign * math.sin(2 * math.pi * k / n)
    if 8 * k == n:
        return c * (re - sign * im), c * (im + sign * re)
    if 8 * k == 3 * n:
        return c * (re + sign * im), c * (im - sign * re)
    return c * re - s * im, c * im + s * re


def real_transform(x):
    n = len(x)
    if n == 2:
        return [(x[0] + x[1], None), (x[0] - x[1], None)]
    even, odd = real_transform(x[0::2]), real_transform(x[1::2])
    out = [None] * (n // 2 + 1)
    out[0] = (even[0][0] + odd[0][0], None)
    out[n // 2] = (even[0][0] - odd[0][0], None)
    out[n // 4] = (even[n // 4][0], -odd[n // 4][0])
    for k in range(1, n // 4):
        re, im = turn(*odd[k], k, n, -1)
        out[k] = (even[k][0] + re, even[k][1] + im)
        out[n // 2 - k] = (even[k][0] - re, im - even[k][1])
    return out


def real_inverse(spectrum):
    n = 2 * (len(spectrum) - 1)
    if n == 2:
        return [spectrum[0][0] + spectrum[1][0], spectrum[0][0] - spectrum[1][0]]
    even, odd = [None] * (n // 4 + 1), [None] * (n // 4 + 1)
    even[0] = (spectrum[0][0] + spectrum[n // 2][0], None)
    odd[0] = (spectrum[0][0] - spectrum[n // 2][0], None)
    even[n // 4] = (2.0 * spectrum[n // 4][0], None)
    odd[n // 4] = (-2.0 * spectrum[n // 4][1], None)
    for k in range(1, n // 4):
        (re, im), (re_far, im_far) = spectrum[k], spectrum[n // 2 - k]
        even[k] = (re + re_far, im - im_far)
        odd[k] = turn(re - re_far, im + im_far, k, n, 1)
    out = [None] * n
    out[0::2], out[1::2] = real_inverse(even), real_inverse(odd)
    return out


C1, C2 = math.cos(2 * math.pi / 5), math.cos(4 * math.pi / 5)
S1, S2 = math.sin(2 * math.pi / 5), math.sin(4 * math.pi / 5)


def five_parts(x):
    t1, t2, t3, t4 = x[1] + x[4], x[2] + x[3], x[1] - x[4], x[2] - x[3]
    return (
        x[0] + t1 + t2,
        x[0] + C1 * t1 + C2 * t2,
        x[0] + C2 * t1 + C1 * t2,
        S1 * t3 + S2 * t4,
        S2 * t3 - S1 * t4,
    )


def five_real(x, kernel):
    zero, a1, a2, b1, b2 = five_parts(x)
    zero, a1, a2, b1, b2 = kernel[0] * zero, 2.0 * kernel[1] * a1, 2.0 * kernel[2] * a2, 2.0 * kernel[1] * b1, 2.0 * kernel[2] * b2
    m1, m2 = zero + C1 * a1 + C2 * a2, zero + C2 * a1 + C1 * a2
    n1, n2 = S1 * b1 + S2 * b2, S2 * b1 - S1 * b2
    return [zero + a1 + a2, m1 + n1, m2 + n2, m2 - n2, m1 - n1]


def five_complex(re, im, kernel):
    r0, ra1, ra2, rb1, rb2 = five_parts(re)
    i0, ia1, ia2, ib1, ib2 = five_parts(im)
    r = [kernel[0] * r0, kernel[1] * (ra1 + ib1), kernel[2] * (ra2 + ib2), kernel[3] * (ra2 - ib2), kernel[4] * (ra1 - ib1)]
    i = [kernel[0] * i0, kernel[1] * (ia1 - rb1), kernel[2] * (ia2 - rb2), kernel[3] * (ia2 + rb2), kernel[4] * (ia1 + rb1)]
    r0, ra1, ra2, rb1, rb2 = five_parts(r)
    i0, ia1, ia2, ib1, ib2 = five_parts(i)
    return (
        [r0, ra1 - ib1, ra2 - ib2, ra2 + ib2, ra1 + ib1],
        [i0, ia1 + rb1, ia2 + rb2, ia2 - rb2, ia1 - rb1],
    )


def times(table, data):
    high = data.astype(BF16)
    low = (data - high.astype(F32)).astype(BF16)
    stacked = jnp.concatenate([high, low, high], axis=0)
    return lax.dot_general(table, stacked, (((1,), (0,)), ((), ())), preferred_element_type=F32)


def piece(data, index):
    return data[:, LANES * index : LANES * (index + 1)]


def unit_body(near_a, near_b, far_a, far_b, table_y, table_to, table_from, kernel, total, out, done, there, back, mid, turned):
    done[0, 0] = 0
    fill = jnp.zeros((LANES - N, LANES), F32)

    def forward_y(a, b, first, group):
        start = group * PLANES
        density = jnp.concatenate([a[start + i] * b[start + i] for i in range(PLANES)], axis=1)
        along_y = times(table_y[...], density)
        for i in range(PLANES):
            turned[first + start + i] = jnp.concatenate([piece(along_y, i), fill], axis=0).T

    def forward_z(group):
        start = group * PLANES
        rows = [
            jnp.concatenate(
                [
                    turned[start + j // 2, LOW * (j % 2) : LOW * (j % 2) + LOW],
                    turned[start + 4, HIGH * j : HIGH * (j + 1)],
                ],
                axis=0,
            )
            for j in range(GROUP)
        ]
        along_z = times(table_to[...], jnp.concatenate(rows, axis=1))
        for j in range(GROUP):
            there[group * GROUP + j] = piece(along_z, j)

    def middle(group, kernel_group):
        rows = pl.ds(pl.multiple_of(group * GROUP, GROUP), GROUP)
        for n2 in range(5):
            for k1, (re, im) in enumerate(real_transform([there[point(n1, n2), rows, :] for n1 in range(16)])):
                mid[2 * k1, n2] = re
                if im is not None:
                    mid[2 * k1 + 1, n2] = im
        for k1 in range(9):
            scale = [kernel[kernel_group, frequency(k1, k2)] for k2 in range(5)]
            re = [mid[2 * k1, n2] for n2 in range(5)]
            if k1 in (0, 8):
                re = five_real(re, scale)
            else:
                re, im = five_complex(re, [mid[2 * k1 + 1, n2] for n2 in range(5)], scale)
                for n2 in range(5):
                    mid[2 * k1 + 1, n2] = im[n2]
            for n2 in range(5):
                mid[2 * k1, n2] = re[n2]
        for n2 in range(5):
            spectrum = [(mid[2 * k1, n2], None if k1 in (0, 8) else mid[2 * k1 + 1, n2]) for k1 in range(9)]
            for n1, value in enumerate(real_inverse(spectrum)):
                if point(n1, n2) < HALF:
                    back[point(n1, n2), rows, :] = value

    def backward_z(group):
        rows = [back[group * GROUP + j] for j in range(GROUP)]
        along_z = times(table_from[...], jnp.concatenate(rows, axis=1))
        parts = [piece(along_z, j) for j in range(GROUP)]
        packed = [jnp.concatenate([parts[2 * i][:LOW], parts[2 * i + 1][:LOW]], axis=0) for i in range(4)]
        packed.append(jnp.concatenate([part[LOW:] for part in parts], axis=0))
        for i, plane in enumerate(packed):
            turned[group * PLANES + i] = plane.T

    def backward_y(group):
        start = group * PLANES
        planes = jnp.concatenate([turned[start + i, :N] for i in range(PLANES)], axis=1)
        potential = times(table_y[...], planes)
        for i in range(PLANES):
            term = piece(potential, i) * near_b[start + i]
            out[start + i] = term if total is None else total[start + i] + term

    for group in range(GROUPS):
        forward_y(near_a, near_b, 0, group)
        forward_y(far_a, far_b, GROUPS * PLANES, group)
    for group in range(2 * GROUPS):
        forward_z(group)

    @pl.loop(0, 2 * GROUPS)
    def _(group):
        middle(group, jnp.where(group > GROUPS, group - GROUPS, group))

    for group in range(GROUPS):
        backward_z(group)
    for group in range(GROUPS):
        backward_y(group)


def unit(a, b, constants, after, total=None, waits=(), again=False):
    operands = [a[0], b[0], a[1], b[1], *constants]

    def body(order, *refs):
        refs = list(refs[len(waits) :])
        if again:
            copied = refs.pop(len(operands) + (total is not None) + 2)

            @pl.loop(0, GROUPS * PLANES)
            def _(plane):
                copied[plane] = refs[2][plane]

        ins, rest = refs[: len(operands)], refs[len(operands) :]
        if total is None:
            unit_body(*ins, None, *rest)
        else:
            unit_body(*ins, *rest)

    here = pl.BlockSpec(memory_space=pltpu.VMEM)
    scalar = pl.BlockSpec(memory_space=pltpu.SMEM)
    operands_all = (*operands, *(() if total is None else (total,)))
    return pl.pallas_call(
        body,
        in_specs=[scalar] + [pl.BlockSpec(memory_space=pl.ANY)] * len(waits) + [here] * len(operands_all),
        out_specs=(here, scalar) + (here,) * again,
        out_shape=(jax.ShapeDtypeStruct(PACKED, F32), jax.ShapeDtypeStruct((1, 1), jnp.int32))
        + (jax.ShapeDtypeStruct(PACKED, F32),) * again,
        scratch_shapes=[
            pltpu.VMEM((N, N, LANES), F32),
            pltpu.VMEM((HALF, N, LANES), F32),
            pltpu.VMEM((17, 5, GROUP, LANES), F32),
            pltpu.VMEM((2 * GROUPS * PLANES, LANES, LANES), F32),
        ],
        compiler_params=pltpu.CompilerParams(vmem_limit_bytes=20 * 2**20),
        cost_estimate=pl.CostEstimate(flops=1, bytes_accessed=1, transcendentals=0),
        name="unit",
    )(after, *waits, *operands_all)


def choose_body(places, order, a, b, out):
    place = lax.axis_index("band")
    takes = functools.reduce(jnp.logical_or, [place == p for p in places])

    @pl.when(takes)
    def _():
        @pl.loop(0, GROUPS * PLANES)
        def _(plane):
            out[plane] = a[plane]

    @pl.when(jnp.logical_not(takes))
    def _():
        @pl.loop(0, GROUPS * PLANES)
        def _(plane):
            out[plane] = b[plane]


def choose(places, a, b, after):
    here = pl.BlockSpec(memory_space=pltpu.VMEM)
    return pl.pallas_call(
        functools.partial(choose_body, places),
        in_specs=[pl.BlockSpec(memory_space=pltpu.SMEM), here, here],
        out_specs=here,
        out_shape=jax.ShapeDtypeStruct(PACKED, F32),
        compiler_params=pltpu.CompilerParams(vmem_limit_bytes=8 * 2**20),
        cost_estimate=pl.CostEstimate(flops=1, bytes_accessed=1, transcendentals=0),
        name="choose",
    )(after, a, b)


def pack_body(data, out):
    lane = lax.broadcasted_iota(jnp.int32, (N, LANES), 1)
    pad = jnp.zeros((N, LANES - N), F32)

    @pl.loop(0, GROUPS)
    def _(group):
        last = None
        for i in range(4):
            pair = [jnp.concatenate([data[group * GROUP + 2 * i + h], pad], axis=1) for h in range(2)]
            out[group * PLANES + i] = jnp.where(lane < LOW, pair[0], pltpu.roll(pair[1], LOW, 1))
            for h in range(2):
                place = HIGH * (2 * i + h)
                moved = pltpu.roll(pair[h], (place - LOW) % LANES, 1) if place != LOW else pair[h]
                last = moved if last is None else jnp.where(lane >= place, moved, last)
        out[group * PLANES + 4] = last


def pack(data):
    return pl.pallas_call(
        pack_body,
        out_shape=jax.ShapeDtypeStruct(PACKED, F32),
        compiler_params=pltpu.CompilerParams(vmem_limit_bytes=16 * 2**20),
        name="pack",
    )(data)


def unpack_body(total, returned, theirs, out):
    lane = lax.broadcasted_iota(jnp.int32, (N, LANES), 1)

    @pl.loop(0, GROUPS)
    def _(group):
        start = group * PLANES
        planes = [total[start + i] + returned[start + i] + theirs[start + i] for i in range(PLANES)]
        for j in range(GROUP):
            low = planes[j // 2] if j % 2 == 0 else pltpu.roll(planes[j // 2], LOW, 1)
            place = HIGH * j
            high = pltpu.roll(planes[4], (LOW - place) % LANES, 1) if place != LOW else planes[4]
            out[group * GROUP + j] = jnp.where(lane < LOW, low, high)[:, :N]


def unpack_sum(total, returned, theirs):
    return pl.pallas_call(
        unpack_body,
        out_shape=jax.ShapeDtypeStruct((HALF, N, N), F32),
        compiler_params=pltpu.CompilerParams(vmem_limit_bytes=16 * 2**20),
        name="unpack_sum",
    )(total, returned, theirs)


def shards(orbitals):
    bands = lax.axis_size("band")
    half = bands // 2
    sides = [1 if b % 2 else -1 for b in range(bands)]

    def sources(distance):
        return [(b + distance * sides[b]) % bands for b in range(bands)]

    def crosses(b, source):
        return b // half != source // half

    def from_place(data, distance):
        return lax.ppermute(data, "band", [(source, b) for b, source in enumerate(sources(distance))])

    def near_inside(data, distance):
        return lax.ppermute(
            data, "band", [(source, b) for b, source in enumerate(sources(distance)) if not crosses(b, source)]
        )

    def across(distance):
        return [(source, b) for b, source in enumerate(sources(distance)) if crosses(b, source)]

    def other_core(data):
        return from_place(data, -1)

    constants = tuple(jnp.asarray(t) for t in (*tables(), screened_kernel()))
    near = pack(orbitals[0])
    far = lax.ppermute(near, "grid", [(0, 1), (1, 0)])
    m2_inside = near_inside(near, -2)
    p2_inside = near_inside(near, 2)
    p2_inside, m2_inside, far = lax.optimization_barrier((p2_inside, m2_inside, far))
    own = (near, far)
    m2_far = from_place(far, -2)
    crossed = lax.ppermute(
        far, ("band", "grid"), [(2 * a + 1 - slab, 2 * b + slab) for a, b in across(-2) + across(2) for slab in range(2)]
    )
    m2_takes, p2_takes = ([b for _, b in across(distance)] for distance in (-2, 2))
    m1 = (other_core(near), other_core(far))
    first = jnp.zeros((1, 1), jnp.int32)
    total, after, far_later = unit(own, m1, constants, first, waits=(m2_inside, p2_inside), again=True)
    p2_far = from_place(far_later, 2)
    m2_far, after = lax.optimization_barrier((m2_far, after))
    m2 = (choose(m2_takes, crossed, m2_inside, after), m2_far)
    p1 = (other_core(m2[0]), other_core(m2_far))
    total, after = unit(own, m2, constants, after, total)
    lent, after = unit(m2, p1, constants, after)
    returned = from_place(lent, 2)
    partner, after = unit(m1, m2, constants, after, waits=(p2_far,))
    p2 = (choose(p2_takes, crossed, p2_inside, after), p2_far)
    partner, after = unit(m1, p2, constants, after, partner)
    theirs = other_core(partner)
    total, after = unit(own, p2, constants, after, total, waits=(returned,))
    return unpack_sum(total, returned, theirs)[None]


def solution(mesh):
    spec = P("band", "grid", None, None)
    return jax.shard_map(shards, mesh=mesh, in_specs=(spec,), out_specs=spec, check_vma=False)
```

```python
import functools
import math

import jax
import jax.numpy as jnp
import numpy as np
from jax import lax
from jax.experimental import pallas as pl
from jax.experimental.pallas import tpu as pltpu
from jax.sharding import PartitionSpec as P

CELL_LENGTH = 37.2
SCREENING = 0.106
BF16 = jnp.bfloat16
F32 = jnp.float32
N = 80
HALF = N // 2
GROUP = 8
GROUPS = HALF // GROUP
PLANES = 5
PACKED = (GROUPS * PLANES, N, 128)
LANES = 128
LOW, HIGH = 64, 16

FOLD = np.concatenate([np.arange(HALF), [HALF], np.arange(N - 1, HALF, -1)])


def cas(rows, columns):
    angles = (rows[:, None] * columns[None, :] % N) * (2.0 * math.pi / N)
    return np.cos(angles) + np.sin(angles)


def three_terms(table):
    high = table.astype(np.float32).astype(jnp.bfloat16)
    low = (table - high.astype(np.float64)).astype(np.float32).astype(jnp.bfloat16)
    return np.concatenate([high, high, low], axis=1)


def tables():
    places = np.arange(N)
    return (
        three_terms(cas(places, places)),
        three_terms(cas(FOLD, places)),
        three_terms(cas(places, FOLD)),
    )


def screened_kernel():
    line = np.arange(N)
    freq_y = np.pad(np.where(2 * line >= N, line - N, line), (0, LANES - N))[None, None, None, :]
    freq_x = np.arange(HALF + 1)[None, :, None, None]
    freq_z = np.concatenate([np.arange(HALF + 1), np.arange(1, GROUP)]).reshape(6, 1, GROUP, 1)
    squares = freq_x * freq_x + freq_y * freq_y + freq_z * freq_z
    wave_square = np.where(squares == 0, 1, squares) * (2.0 * math.pi / CELL_LENGTH) ** 2
    shaped = 4.0 * math.pi / wave_square * (1.0 - np.exp(-wave_square / (4.0 * SCREENING**2)))
    return (np.where(squares == 0, math.pi / SCREENING**2, shaped) * (1.0 / N**3)).astype(np.float32)


def point(n1, n2):
    return (5 * n1 + 16 * n2) % N


def frequency(k1, k2):
    k = next(k for k in range(N) if k % 16 == k1 and k % 5 == k2)
    return min(k, N - k)


def turn(re, im, k, n, sign):
    if k == 0:
        return re, im
    if 4 * k == n:
        return (-im, re) if sign > 0 else (im, -re)
    c, s = math.cos(2 * math.pi * k / n), sign * math.sin(2 * math.pi * k / n)
    if 8 * k == n:
        return c * (re - sign * im), c * (im + sign * re)
    if 8 * k == 3 * n:
        return c * (re + sign * im), c * (im - sign * re)
    return c * re - s * im, c * im + s * re


def real_transform(x):
    n = len(x)
    if n == 2:
        return [(x[0] + x[1], None), (x[0] - x[1], None)]
    even, odd = real_transform(x[0::2]), real_transform(x[1::2])
    out = [None] * (n // 2 + 1)
    out[0] = (even[0][0] + odd[0][0], None)
    out[n // 2] = (even[0][0] - odd[0][0], None)
    out[n // 4] = (even[n // 4][0], -odd[n // 4][0])
    for k in range(1, n // 4):
        re, im = turn(*odd[k], k, n, -1)
        out[k] = (even[k][0] + re, even[k][1] + im)
        out[n // 2 - k] = (even[k][0] - re, im - even[k][1])
    return out


def real_inverse(spectrum):
    n = 2 * (len(spectrum) - 1)
    if n == 2:
        return [spectrum[0][0] + spectrum[1][0], spectrum[0][0] - spectrum[1][0]]
    even, odd = [None] * (n // 4 + 1), [None] * (n // 4 + 1)
    even[0] = (spectrum[0][0] + spectrum[n // 2][0], None)
    odd[0] = (spectrum[0][0] - spectrum[n // 2][0], None)
    even[n // 4] = (2.0 * spectrum[n // 4][0], None)
    odd[n // 4] = (-2.0 * spectrum[n // 4][1], None)
    for k in range(1, n // 4):
        (re, im), (re_far, im_far) = spectrum[k], spectrum[n // 2 - k]
        even[k] = (re + re_far, im - im_far)
        odd[k] = turn(re - re_far, im + im_far, k, n, 1)
    out = [None] * n
    out[0::2], out[1::2] = real_inverse(even), real_inverse(odd)
    return out


C1, C2 = math.cos(2 * math.pi / 5), math.cos(4 * math.pi / 5)
S1, S2 = math.sin(2 * math.pi / 5), math.sin(4 * math.pi / 5)


def five_parts(x):
    t1, t2, t3, t4 = x[1] + x[4], x[2] + x[3], x[1] - x[4], x[2] - x[3]
    return (
        x[0] + t1 + t2,
        x[0] + C1 * t1 + C2 * t2,
        x[0] + C2 * t1 + C1 * t2,
        S1 * t3 + S2 * t4,
        S2 * t3 - S1 * t4,
    )


def five_real(x, kernel):
    zero, a1, a2, b1, b2 = five_parts(x)
    zero, a1, a2, b1, b2 = kernel[0] * zero, 2.0 * kernel[1] * a1, 2.0 * kernel[2] * a2, 2.0 * kernel[1] * b1, 2.0 * kernel[2] * b2
    m1, m2 = zero + C1 * a1 + C2 * a2, zero + C2 * a1 + C1 * a2
    n1, n2 = S1 * b1 + S2 * b2, S2 * b1 - S1 * b2
    return [zero + a1 + a2, m1 + n1, m2 + n2, m2 - n2, m1 - n1]


def five_complex(re, im, kernel):
    r0, ra1, ra2, rb1, rb2 = five_parts(re)
    i0, ia1, ia2, ib1, ib2 = five_parts(im)
    r = [kernel[0] * r0, kernel[1] * (ra1 + ib1), kernel[2] * (ra2 + ib2), kernel[3] * (ra2 - ib2), kernel[4] * (ra1 - ib1)]
    i = [kernel[0] * i0, kernel[1] * (ia1 - rb1), kernel[2] * (ia2 - rb2), kernel[3] * (ia2 + rb2), kernel[4] * (ia1 + rb1)]
    r0, ra1, ra2, rb1, rb2 = five_parts(r)
    i0, ia1, ia2, ib1, ib2 = five_parts(i)
    return (
        [r0, ra1 - ib1, ra2 - ib2, ra2 + ib2, ra1 + ib1],
        [i0, ia1 + rb1, ia2 + rb2, ia2 - rb2, ia1 - rb1],
    )


def times(table, data):
    high = data.astype(BF16)
    low = (data - high.astype(F32)).astype(BF16)
    stacked = jnp.concatenate([high, low, high], axis=0)
    return lax.dot_general(table, stacked, (((1,), (0,)), ((), ())), preferred_element_type=F32)


def piece(data, index):
    return data[:, LANES * index : LANES * (index + 1)]


def unit_body(near_a, near_b, far_a, far_b, table_y, table_to, table_from, kernel, total, out, done, there, back, mid, turned):
    done[0, 0] = 0
    fill = jnp.zeros((LANES - N, LANES), F32)

    def forward_y(a, b, first, group):
        start = group * PLANES
        density = jnp.concatenate([a[start + i] * b[start + i] for i in range(PLANES)], axis=1)
        along_y = times(table_y[...], density)
        for i in range(PLANES):
            turned[first + start + i] = jnp.concatenate([piece(along_y, i), fill], axis=0).T

    def forward_z(group):
        start = group * PLANES
        rows = [
            jnp.concatenate(
                [
                    turned[start + j // 2, LOW * (j % 2) : LOW * (j % 2) + LOW],
                    turned[start + 4, HIGH * j : HIGH * (j + 1)],
                ],
                axis=0,
            )
            for j in range(GROUP)
        ]
        along_z = times(table_to[...], jnp.concatenate(rows, axis=1))
        for j in range(GROUP):
            there[group * GROUP + j] = piece(along_z, j)

    def middle(group, kernel_group):
        rows = pl.ds(pl.multiple_of(group * GROUP, GROUP), GROUP)
        for n2 in range(5):
            for k1, (re, im) in enumerate(real_transform([there[point(n1, n2), rows, :] for n1 in range(16)])):
                mid[2 * k1, n2] = re
                if im is not None:
                    mid[2 * k1 + 1, n2] = im
        for k1 in range(9):
            scale = [kernel[kernel_group, frequency(k1, k2)] for k2 in range(5)]
            re = [mid[2 * k1, n2] for n2 in range(5)]
            if k1 in (0, 8):
                re = five_real(re, scale)
            else:
                re, im = five_complex(re, [mid[2 * k1 + 1, n2] for n2 in range(5)], scale)
                for n2 in range(5):
                    mid[2 * k1 + 1, n2] = im[n2]
            for n2 in range(5):
                mid[2 * k1, n2] = re[n2]
        for n2 in range(5):
            spectrum = [(mid[2 * k1, n2], None if k1 in (0, 8) else mid[2 * k1 + 1, n2]) for k1 in range(9)]
            for n1, value in enumerate(real_inverse(spectrum)):
                if point(n1, n2) < HALF:
                    back[point(n1, n2), rows, :] = value

    def backward_z(group):
        rows = [back[group * GROUP + j] for j in range(GROUP)]
        along_z = times(table_from[...], jnp.concatenate(rows, axis=1))
        parts = [piece(along_z, j) for j in range(GROUP)]
        packed = [jnp.concatenate([parts[2 * i][:LOW], parts[2 * i + 1][:LOW]], axis=0) for i in range(4)]
        packed.append(jnp.concatenate([part[LOW:] for part in parts], axis=0))
        for i, plane in enumerate(packed):
            turned[group * PLANES + i] = plane.T

    def backward_y(group):
        start = group * PLANES
        planes = jnp.concatenate([turned[start + i, :N] for i in range(PLANES)], axis=1)
        potential = times(table_y[...], planes)
        for i in range(PLANES):
            term = piece(potential, i) * near_b[start + i]
            out[start + i] = term if total is None else total[start + i] + term

    for group in range(GROUPS):
        forward_y(near_a, near_b, 0, group)
        forward_y(far_a, far_b, GROUPS * PLANES, group)
    for group in range(2 * GROUPS):
        forward_z(group)

    @pl.loop(0, 2 * GROUPS)
    def _(group):
        middle(group, jnp.where(group > GROUPS, group - GROUPS, group))

    for group in range(GROUPS):
        backward_z(group)
    for group in range(GROUPS):
        backward_y(group)


def unit(a, b, constants, after, total=None, waits=()):
    operands = [a[0], b[0], a[1], b[1], *constants]

    def body(order, *refs):
        refs = refs[len(waits) :]
        ins, rest = refs[: len(operands)], refs[len(operands) :]
        if total is None:
            unit_body(*ins, None, *rest)
        else:
            unit_body(*ins, *rest)

    here = pl.BlockSpec(memory_space=pltpu.VMEM)
    scalar = pl.BlockSpec(memory_space=pltpu.SMEM)
    operands_all = (*operands, *(() if total is None else (total,)))
    return pl.pallas_call(
        body,
        in_specs=[scalar] + [pl.BlockSpec(memory_space=pl.ANY)] * len(waits) + [here] * len(operands_all),
        out_specs=(here, scalar),
        out_shape=(jax.ShapeDtypeStruct(PACKED, F32), jax.ShapeDtypeStruct((1, 1), jnp.int32)),
        scratch_shapes=[
            pltpu.VMEM((N, N, LANES), F32),
            pltpu.VMEM((HALF, N, LANES), F32),
            pltpu.VMEM((17, 5, GROUP, LANES), F32),
            pltpu.VMEM((2 * GROUPS * PLANES, LANES, LANES), F32),
        ],
        compiler_params=pltpu.CompilerParams(vmem_limit_bytes=20 * 2**20),
        cost_estimate=pl.CostEstimate(flops=1, bytes_accessed=1, transcendentals=0),
        name="unit",
    )(after, *waits, *operands_all)


def choose_body(places, order, a, b, out):
    place = lax.axis_index("band")
    takes = functools.reduce(jnp.logical_or, [place == p for p in places])

    @pl.when(takes)
    def _():
        @pl.loop(0, GROUPS * PLANES)
        def _(plane):
            out[plane] = a[plane]

    @pl.when(jnp.logical_not(takes))
    def _():
        @pl.loop(0, GROUPS * PLANES)
        def _(plane):
            out[plane] = b[plane]


def choose(places, a, b, after):
    here = pl.BlockSpec(memory_space=pltpu.VMEM)
    return pl.pallas_call(
        functools.partial(choose_body, places),
        in_specs=[pl.BlockSpec(memory_space=pltpu.SMEM), here, here],
        out_specs=here,
        out_shape=jax.ShapeDtypeStruct(PACKED, F32),
        compiler_params=pltpu.CompilerParams(vmem_limit_bytes=8 * 2**20),
        cost_estimate=pl.CostEstimate(flops=1, bytes_accessed=1, transcendentals=0),
        name="choose",
    )(after, a, b)


def pack_body(data, out):
    lane = lax.broadcasted_iota(jnp.int32, (N, LANES), 1)
    pad = jnp.zeros((N, LANES - N), F32)

    @pl.loop(0, GROUPS)
    def _(group):
        last = None
        for i in range(4):
            pair = [jnp.concatenate([data[group * GROUP + 2 * i + h], pad], axis=1) for h in range(2)]
            out[group * PLANES + i] = jnp.where(lane < LOW, pair[0], pltpu.roll(pair[1], LOW, 1))
            for h in range(2):
                place = HIGH * (2 * i + h)
                moved = pltpu.roll(pair[h], (place - LOW) % LANES, 1) if place != LOW else pair[h]
                last = moved if last is None else jnp.where(lane >= place, moved, last)
        out[group * PLANES + 4] = last


def pack(data):
    return pl.pallas_call(
        pack_body,
        out_shape=jax.ShapeDtypeStruct(PACKED, F32),
        compiler_params=pltpu.CompilerParams(vmem_limit_bytes=16 * 2**20),
        name="pack",
    )(data)


def unpack_body(total, returned, theirs, out):
    lane = lax.broadcasted_iota(jnp.int32, (N, LANES), 1)

    @pl.loop(0, GROUPS)
    def _(group):
        start = group * PLANES
        planes = [total[start + i] + returned[start + i] + theirs[start + i] for i in range(PLANES)]
        for j in range(GROUP):
            low = planes[j // 2] if j % 2 == 0 else pltpu.roll(planes[j // 2], LOW, 1)
            place = HIGH * j
            high = pltpu.roll(planes[4], (LOW - place) % LANES, 1) if place != LOW else planes[4]
            out[group * GROUP + j] = jnp.where(lane < LOW, low, high)[:, :N]


def unpack_sum(total, returned, theirs):
    return pl.pallas_call(
        unpack_body,
        out_shape=jax.ShapeDtypeStruct((HALF, N, N), F32),
        compiler_params=pltpu.CompilerParams(vmem_limit_bytes=16 * 2**20),
        name="unpack_sum",
    )(total, returned, theirs)


def shards(orbitals):
    bands = lax.axis_size("band")
    half = bands // 2
    sides = [1 if b % 2 else -1 for b in range(bands)]

    def sources(distance):
        return [(b + distance * sides[b]) % bands for b in range(bands)]

    def takers(distance):
        return [b for b, source in enumerate(sources(distance)) if b // half != source // half]

    def from_place(data, distance):
        return lax.ppermute(data, "band", [(source, b) for b, source in enumerate(sources(distance))])

    def from_half(data, distance):
        return lax.ppermute(data, "band", [(b // half * half + source % half, b) for b, source in enumerate(sources(distance))])

    def swapped_halves(data, distance):
        return lax.ppermute(data, "band", [((b + half) % bands, b) for b in takers(distance)])

    def far_slabs(near, far, distance, after):
        route = []
        for b, source in enumerate(sources(distance)):
            for slab in range(2):
                route.append((2 * source + (1 - slab if b in takers(distance) else slab), 2 * b + slab))
        across = [sources(distance)[b] for b in takers(distance)]
        return lax.ppermute(choose(across, near, far, after), ("band", "grid"), route)

    def other_core(data):
        return from_place(data, -1)

    constants = tuple(jnp.asarray(t) for t in (*tables(), screened_kernel()))
    near = pack(orbitals[0])
    far = lax.ppermute(near, "grid", [(0, 1), (1, 0)])
    m2_half = from_half(near, -2)
    p2_half = from_half(near, 2)
    far, m2_half, p2_half = lax.optimization_barrier((far, m2_half, p2_half))
    own = (near, far)
    first = jnp.zeros((1, 1), jnp.int32)
    m2_far = far_slabs(near, far, -2, first)
    m2_swapped = swapped_halves(m2_half, -2)
    m1 = (other_core(near), other_core(far))
    total, after = unit(own, m1, constants, first)
    p2_far = far_slabs(near, far, 2, after)
    m2_far, p2_half, after = lax.optimization_barrier((m2_far, p2_half, after))
    p2_swapped = swapped_halves(p2_half, 2)
    m2 = (choose(takers(-2), m2_swapped, m2_half, after), m2_far)
    p1 = (other_core(m2[0]), other_core(m2_far))
    total, after = unit(own, m2, constants, after, total)
    lent, after = unit(m2, p1, constants, after)
    returned = from_place(lent, 2)
    partner, after = unit(m1, m2, constants, after, waits=(p2_far,))
    p2 = (choose(takers(2), p2_swapped, p2_half, after), p2_far)
    partner, after = unit(m1, p2, constants, after, partner)
    theirs = other_core(partner)
    total, after = unit(own, p2, constants, after, total, waits=(returned,))
    return unpack_sum(total, returned, theirs)[None]


def solution(mesh):
    spec = P("band", "grid", None, None)
    return jax.shard_map(shards, mesh=mesh, in_specs=(spec,), out_specs=spec, check_vma=False)
```

```python
import functools
import math

import jax
import jax.numpy as jnp
import numpy as np
from jax import lax
from jax.experimental import pallas as pl
from jax.experimental.pallas import tpu as pltpu
from jax.sharding import PartitionSpec as P

CELL_LENGTH = 37.2
SCREENING = 0.106
BF16 = jnp.bfloat16
F32 = jnp.float32
N = 80
HALF = N // 2
GROUP = 8
GROUPS = HALF // GROUP
PLANES = 5
PACKED = (GROUPS * PLANES, N, 128)
LANES = 128
LOW, HIGH = 64, 16

FOLD = np.concatenate([np.arange(HALF), [HALF], np.arange(N - 1, HALF, -1)])


def cas(rows, columns):
    angles = (rows[:, None] * columns[None, :] % N) * (2.0 * math.pi / N)
    return np.cos(angles) + np.sin(angles)


def three_terms(table):
    high = table.astype(np.float32).astype(jnp.bfloat16)
    low = (table - high.astype(np.float64)).astype(np.float32).astype(jnp.bfloat16)
    return np.concatenate([high, high, low], axis=1)


def tables():
    places = np.arange(N)
    return (
        three_terms(cas(places, places)),
        three_terms(cas(FOLD, places)),
        three_terms(cas(places, FOLD)),
    )


def screened_kernel():
    line = np.arange(N)
    freq_y = np.pad(np.where(2 * line >= N, line - N, line), (0, LANES - N))[None, None, None, :]
    freq_x = np.arange(HALF + 1)[None, :, None, None]
    freq_z = np.concatenate([np.arange(HALF + 1), np.arange(1, GROUP)]).reshape(6, 1, GROUP, 1)
    squares = freq_x * freq_x + freq_y * freq_y + freq_z * freq_z
    wave_square = np.where(squares == 0, 1, squares) * (2.0 * math.pi / CELL_LENGTH) ** 2
    shaped = 4.0 * math.pi / wave_square * (1.0 - np.exp(-wave_square / (4.0 * SCREENING**2)))
    return (np.where(squares == 0, math.pi / SCREENING**2, shaped) * (1.0 / N**3)).astype(np.float32)


def point(n1, n2):
    return (5 * n1 + 16 * n2) % N


def frequency(k1, k2):
    k = next(k for k in range(N) if k % 16 == k1 and k % 5 == k2)
    return min(k, N - k)


def turn(re, im, k, n, sign):
    if k == 0:
        return re, im
    if 4 * k == n:
        return (-im, re) if sign > 0 else (im, -re)
    c, s = math.cos(2 * math.pi * k / n), sign * math.sin(2 * math.pi * k / n)
    if 8 * k == n:
        return c * (re - sign * im), c * (im + sign * re)
    if 8 * k == 3 * n:
        return c * (re + sign * im), c * (im - sign * re)
    return c * re - s * im, c * im + s * re


def real_transform(x):
    n = len(x)
    if n == 2:
        return [(x[0] + x[1], None), (x[0] - x[1], None)]
    even, odd = real_transform(x[0::2]), real_transform(x[1::2])
    out = [None] * (n // 2 + 1)
    out[0] = (even[0][0] + odd[0][0], None)
    out[n // 2] = (even[0][0] - odd[0][0], None)
    out[n // 4] = (even[n // 4][0], -odd[n // 4][0])
    for k in range(1, n // 4):
        re, im = turn(*odd[k], k, n, -1)
        out[k] = (even[k][0] + re, even[k][1] + im)
        out[n // 2 - k] = (even[k][0] - re, im - even[k][1])
    return out


def real_inverse(spectrum):
    n = 2 * (len(spectrum) - 1)
    if n == 2:
        return [spectrum[0][0] + spectrum[1][0], spectrum[0][0] - spectrum[1][0]]
    even, odd = [None] * (n // 4 + 1), [None] * (n // 4 + 1)
    even[0] = (spectrum[0][0] + spectrum[n // 2][0], None)
    odd[0] = (spectrum[0][0] - spectrum[n // 2][0], None)
    even[n // 4] = (2.0 * spectrum[n // 4][0], None)
    odd[n // 4] = (-2.0 * spectrum[n // 4][1], None)
    for k in range(1, n // 4):
        (re, im), (re_far, im_far) = spectrum[k], spectrum[n // 2 - k]
        even[k] = (re + re_far, im - im_far)
        odd[k] = turn(re - re_far, im + im_far, k, n, 1)
    out = [None] * n
    out[0::2], out[1::2] = real_inverse(even), real_inverse(odd)
    return out


C1, C2 = math.cos(2 * math.pi / 5), math.cos(4 * math.pi / 5)
S1, S2 = math.sin(2 * math.pi / 5), math.sin(4 * math.pi / 5)


def five_parts(x):
    t1, t2, t3, t4 = x[1] + x[4], x[2] + x[3], x[1] - x[4], x[2] - x[3]
    return (
        x[0] + t1 + t2,
        x[0] + C1 * t1 + C2 * t2,
        x[0] + C2 * t1 + C1 * t2,
        S1 * t3 + S2 * t4,
        S2 * t3 - S1 * t4,
    )


def five_real(x, kernel):
    zero, a1, a2, b1, b2 = five_parts(x)
    zero, a1, a2, b1, b2 = kernel[0] * zero, 2.0 * kernel[1] * a1, 2.0 * kernel[2] * a2, 2.0 * kernel[1] * b1, 2.0 * kernel[2] * b2
    m1, m2 = zero + C1 * a1 + C2 * a2, zero + C2 * a1 + C1 * a2
    n1, n2 = S1 * b1 + S2 * b2, S2 * b1 - S1 * b2
    return [zero + a1 + a2, m1 + n1, m2 + n2, m2 - n2, m1 - n1]


def five_complex(re, im, kernel):
    r0, ra1, ra2, rb1, rb2 = five_parts(re)
    i0, ia1, ia2, ib1, ib2 = five_parts(im)
    r = [kernel[0] * r0, kernel[1] * (ra1 + ib1), kernel[2] * (ra2 + ib2), kernel[3] * (ra2 - ib2), kernel[4] * (ra1 - ib1)]
    i = [kernel[0] * i0, kernel[1] * (ia1 - rb1), kernel[2] * (ia2 - rb2), kernel[3] * (ia2 + rb2), kernel[4] * (ia1 + rb1)]
    r0, ra1, ra2, rb1, rb2 = five_parts(r)
    i0, ia1, ia2, ib1, ib2 = five_parts(i)
    return (
        [r0, ra1 - ib1, ra2 - ib2, ra2 + ib2, ra1 + ib1],
        [i0, ia1 + rb1, ia2 + rb2, ia2 - rb2, ia1 - rb1],
    )


def times(table, data):
    high = data.astype(BF16)
    low = (data - high.astype(F32)).astype(BF16)
    stacked = jnp.concatenate([high, low, high], axis=0)
    return lax.dot_general(table, stacked, (((1,), (0,)), ((), ())), preferred_element_type=F32)


def piece(data, index):
    return data[:, LANES * index : LANES * (index + 1)]


def unit_body(near_a, near_b, far_a, far_b, table_y, table_to, table_from, kernel, total, out, done, there, back, mid, turned):
    done[0, 0] = 0
    fill = jnp.zeros((LANES - N, LANES), F32)

    def forward_y(a, b, first, group):
        start = group * PLANES
        density = jnp.concatenate([a[start + i] * b[start + i] for i in range(PLANES)], axis=1)
        along_y = times(table_y[...], density)
        for i in range(PLANES):
            turned[first + start + i] = jnp.concatenate([piece(along_y, i), fill], axis=0).T

    def forward_z(group):
        start = group * PLANES
        rows = [
            jnp.concatenate(
                [
                    turned[start + j // 2, LOW * (j % 2) : LOW * (j % 2) + LOW],
                    turned[start + 4, HIGH * j : HIGH * (j + 1)],
                ],
                axis=0,
            )
            for j in range(GROUP)
        ]
        along_z = times(table_to[...], jnp.concatenate(rows, axis=1))
        for j in range(GROUP):
            there[group * GROUP + j] = piece(along_z, j)

    def middle(group, kernel_group):
        rows = pl.ds(pl.multiple_of(group * GROUP, GROUP), GROUP)
        for n2 in range(5):
            for k1, (re, im) in enumerate(real_transform([there[point(n1, n2), rows, :] for n1 in range(16)])):
                mid[2 * k1, n2] = re
                if im is not None:
                    mid[2 * k1 + 1, n2] = im
        for k1 in range(9):
            scale = [kernel[kernel_group, frequency(k1, k2)] for k2 in range(5)]
            re = [mid[2 * k1, n2] for n2 in range(5)]
            if k1 in (0, 8):
                re = five_real(re, scale)
            else:
                re, im = five_complex(re, [mid[2 * k1 + 1, n2] for n2 in range(5)], scale)
                for n2 in range(5):
                    mid[2 * k1 + 1, n2] = im[n2]
            for n2 in range(5):
                mid[2 * k1, n2] = re[n2]
        for n2 in range(5):
            spectrum = [(mid[2 * k1, n2], None if k1 in (0, 8) else mid[2 * k1 + 1, n2]) for k1 in range(9)]
            for n1, value in enumerate(real_inverse(spectrum)):
                if point(n1, n2) < HALF:
                    back[point(n1, n2), rows, :] = value

    def backward_z(group):
        rows = [back[group * GROUP + j] for j in range(GROUP)]
        along_z = times(table_from[...], jnp.concatenate(rows, axis=1))
        parts = [piece(along_z, j) for j in range(GROUP)]
        packed = [jnp.concatenate([parts[2 * i][:LOW], parts[2 * i + 1][:LOW]], axis=0) for i in range(4)]
        packed.append(jnp.concatenate([part[LOW:] for part in parts], axis=0))
        for i, plane in enumerate(packed):
            turned[group * PLANES + i] = plane.T

    def backward_y(group):
        start = group * PLANES
        planes = jnp.concatenate([turned[start + i, :N] for i in range(PLANES)], axis=1)
        potential = times(table_y[...], planes)
        for i in range(PLANES):
            term = piece(potential, i) * near_b[start + i]
            out[start + i] = term if total is None else total[start + i] + term

    for group in range(GROUPS):
        forward_y(near_a, near_b, 0, group)
        forward_y(far_a, far_b, GROUPS * PLANES, group)
    for group in range(2 * GROUPS):
        forward_z(group)

    @pl.loop(0, 2 * GROUPS)
    def _(group):
        middle(group, jnp.where(group > GROUPS, group - GROUPS, group))

    for group in range(GROUPS):
        backward_z(group)
    for group in range(GROUPS):
        backward_y(group)


def unit(a, b, constants, after, total=None, waits=(), near_at=None):
    operands = [a[0], b[0], a[1], b[1], *constants]

    def body(order, *refs):
        refs = list(refs[len(waits) :])
        if near_at is not None:
            sent = refs.pop(len(operands) + (total is not None) + 2)
            copy_chosen(near_at, refs[0], refs[2], sent)
        ins, rest = refs[: len(operands)], refs[len(operands) :]
        if total is None:
            unit_body(*ins, None, *rest)
        else:
            unit_body(*ins, *rest)

    here = pl.BlockSpec(memory_space=pltpu.VMEM)
    scalar = pl.BlockSpec(memory_space=pltpu.SMEM)
    operands_all = (*operands, *(() if total is None else (total,)))
    return pl.pallas_call(
        body,
        in_specs=[scalar] + [pl.BlockSpec(memory_space=pl.ANY)] * len(waits) + [here] * len(operands_all),
        out_specs=(here, scalar) + (here,) * (near_at is not None),
        out_shape=(jax.ShapeDtypeStruct(PACKED, F32), jax.ShapeDtypeStruct((1, 1), jnp.int32))
        + (jax.ShapeDtypeStruct(PACKED, F32),) * (near_at is not None),
        scratch_shapes=[
            pltpu.VMEM((N, N, LANES), F32),
            pltpu.VMEM((HALF, N, LANES), F32),
            pltpu.VMEM((17, 5, GROUP, LANES), F32),
            pltpu.VMEM((2 * GROUPS * PLANES, LANES, LANES), F32),
        ],
        compiler_params=pltpu.CompilerParams(vmem_limit_bytes=20 * 2**20),
        cost_estimate=pl.CostEstimate(flops=1, bytes_accessed=1, transcendentals=0),
        name="unit",
    )(after, *waits, *operands_all)


def copy_chosen(places, a, b, out):
    place = lax.axis_index("band")
    takes = functools.reduce(jnp.logical_or, [place == p for p in places])

    @pl.when(takes)
    def _():
        @pl.loop(0, GROUPS * PLANES)
        def _(plane):
            out[plane] = a[plane]

    @pl.when(jnp.logical_not(takes))
    def _():
        @pl.loop(0, GROUPS * PLANES)
        def _(plane):
            out[plane] = b[plane]


def choose_body(places, order, a, b, out):
    copy_chosen(places, a, b, out)


def choose(places, a, b, after):
    here = pl.BlockSpec(memory_space=pltpu.VMEM)
    return pl.pallas_call(
        functools.partial(choose_body, places),
        in_specs=[pl.BlockSpec(memory_space=pltpu.SMEM), here, here],
        out_specs=here,
        out_shape=jax.ShapeDtypeStruct(PACKED, F32),
        compiler_params=pltpu.CompilerParams(vmem_limit_bytes=8 * 2**20),
        cost_estimate=pl.CostEstimate(flops=1, bytes_accessed=1, transcendentals=0),
        name="choose",
    )(after, a, b)


def pack_body(data, out):
    lane = lax.broadcasted_iota(jnp.int32, (N, LANES), 1)
    pad = jnp.zeros((N, LANES - N), F32)

    @pl.loop(0, GROUPS)
    def _(group):
        last = None
        for i in range(4):
            pair = [jnp.concatenate([data[group * GROUP + 2 * i + h], pad], axis=1) for h in range(2)]
            out[group * PLANES + i] = jnp.where(lane < LOW, pair[0], pltpu.roll(pair[1], LOW, 1))
            for h in range(2):
                place = HIGH * (2 * i + h)
                moved = pltpu.roll(pair[h], (place - LOW) % LANES, 1) if place != LOW else pair[h]
                last = moved if last is None else jnp.where(lane >= place, moved, last)
        out[group * PLANES + 4] = last


def pack(data):
    return pl.pallas_call(
        pack_body,
        out_shape=jax.ShapeDtypeStruct(PACKED, F32),
        compiler_params=pltpu.CompilerParams(vmem_limit_bytes=16 * 2**20),
        name="pack",
    )(data)


def unpack_body(total, returned, theirs, out, held, sems):
    lane = lax.broadcasted_iota(jnp.int32, (N, LANES), 1)
    copies = []
    for group in range(GROUPS):
        start = group * PLANES
        planes = [total[start + i] + returned[start + i] + theirs[start + i] for i in range(PLANES)]
        for j in range(GROUP):
            low = planes[j // 2] if j % 2 == 0 else pltpu.roll(planes[j // 2], LOW, 1)
            place = HIGH * j
            high = pltpu.roll(planes[4], (LOW - place) % LANES, 1) if place != LOW else planes[4]
            held[group, j] = jnp.where(lane < LOW, low, high)[:, :N]
        copies.append(pltpu.make_async_copy(held.at[group], out.at[pl.ds(group * GROUP, GROUP)], sems.at[group]))
        copies[-1].start()
    for copy in copies:
        copy.wait()


def unpack_sum(total, returned, theirs):
    return pl.pallas_call(
        unpack_body,
        in_specs=[pl.BlockSpec(memory_space=pltpu.VMEM)] * 3,
        out_specs=pl.BlockSpec(memory_space=pltpu.HBM),
        out_shape=jax.ShapeDtypeStruct((HALF, N, N), F32),
        scratch_shapes=[pltpu.VMEM((GROUPS, GROUP, N, N), F32), pltpu.SemaphoreType.DMA((GROUPS,))],
        compiler_params=pltpu.CompilerParams(vmem_limit_bytes=16 * 2**20),
        name="unpack_sum",
    )(total, returned, theirs)


def shards(orbitals):
    bands = lax.axis_size("band")
    half = bands // 2
    sides = [1 if b % 2 else -1 for b in range(bands)]

    def sources(distance):
        return [(b + distance * sides[b]) % bands for b in range(bands)]

    def takers(distance):
        return [b for b, source in enumerate(sources(distance)) if b // half != source // half]

    def from_place(data, distance):
        return lax.ppermute(data, "band", [(source, b) for b, source in enumerate(sources(distance))])

    def from_half(data, distance):
        return lax.ppermute(data, "band", [(b // half * half + source % half, b) for b, source in enumerate(sources(distance))])

    def far_route(distance):
        route = []
        for b, source in enumerate(sources(distance)):
            for slab in range(2):
                route.append((2 * source + (1 - slab if b in takers(distance) else slab), 2 * b + slab))
        return route

    def givers(distance):
        return [sources(distance)[b] for b in takers(distance)]

    def other_core(data):
        return from_place(data, -1)

    constants = tuple(jnp.asarray(t) for t in (*tables(), screened_kernel()))
    near = pack(orbitals[0])
    far = lax.ppermute(near, "grid", [(0, 1), (1, 0)])
    m2_half = from_half(near, -2)
    p2_half = from_half(near, 2)
    p2_half, m2_half, far = lax.optimization_barrier((p2_half, m2_half, far))
    own = (near, far)
    first = jnp.zeros((1, 1), jnp.int32)
    m2_far = lax.ppermute(choose(givers(-2), near, far, first), ("band", "grid"), far_route(-2))
    m1 = (other_core(near), other_core(far))
    swapped = lax.ppermute(
        choose(takers(2), p2_half, m2_half, first), "band", [((b + half) % bands, b) for b in takers(-2) + takers(2)]
    )
    total, after, p2_sent = unit(own, m1, constants, first, near_at=givers(2))
    p2_far = lax.ppermute(p2_sent, ("band", "grid"), far_route(2))
    m2_near = choose(takers(-2), swapped, m2_half, after)
    p1_near = other_core(m2_near)
    m2_far, p1_near, after = lax.optimization_barrier((m2_far, p1_near, after))
    m2 = (m2_near, m2_far)
    p1 = (p1_near, other_core(m2_far))
    total, after = unit(own, m2, constants, after, total)
    lent, after = unit(m2, p1, constants, after)
    returned = from_place(lent, 2)
    partner, after = unit(m1, m2, constants, after, waits=(p2_far,))
    p2 = (choose(takers(2), swapped, p2_half, after), p2_far)
    partner, after = unit(m1, p2, constants, after, partner)
    theirs = other_core(partner)
    total, after = unit(own, p2, constants, after, total, waits=(returned,))
    return unpack_sum(total, returned, theirs)[None]


def solution(mesh):
    spec = P("band", "grid", None, None)
    return jax.shard_map(shards, mesh=mesh, in_specs=(spec,), out_specs=spec, check_vma=False)
```

```python
import functools
import math

import jax
import jax.numpy as jnp
import numpy as np
from jax import lax
from jax.experimental import pallas as pl
from jax.experimental.pallas import tpu as pltpu
from jax.sharding import PartitionSpec as P

CELL_LENGTH = 37.2
SCREENING = 0.106
BF16 = jnp.bfloat16
F32 = jnp.float32
N = 80
HALF = N // 2
GROUP = 8
GROUPS = HALF // GROUP
PLANES = 5
PACKED = (GROUPS * PLANES, N, 128)
LANES = 128
LOW, HIGH = 64, 16

FOLD = np.concatenate([np.arange(HALF), [HALF], np.arange(N - 1, HALF, -1)])


def cas(rows, columns):
    angles = (rows[:, None] * columns[None, :] % N) * (2.0 * math.pi / N)
    return np.cos(angles) + np.sin(angles)


def three_terms(table):
    high = table.astype(np.float32).astype(jnp.bfloat16)
    low = (table - high.astype(np.float64)).astype(np.float32).astype(jnp.bfloat16)
    return np.concatenate([high, high, low], axis=1)


def tables():
    places = np.arange(N)
    return (
        three_terms(cas(places, places)),
        three_terms(cas(FOLD, places)),
        three_terms(cas(places, FOLD)),
    )


def screened_kernel():
    line = np.arange(N)
    freq_y = np.pad(np.where(2 * line >= N, line - N, line), (0, LANES - N))[None, None, None, :]
    freq_x = np.arange(HALF + 1)[None, :, None, None]
    freq_z = np.concatenate([np.arange(HALF + 1), np.arange(1, GROUP)]).reshape(6, 1, GROUP, 1)
    squares = freq_x * freq_x + freq_y * freq_y + freq_z * freq_z
    wave_square = np.where(squares == 0, 1, squares) * (2.0 * math.pi / CELL_LENGTH) ** 2
    shaped = 4.0 * math.pi / wave_square * (1.0 - np.exp(-wave_square / (4.0 * SCREENING**2)))
    return (np.where(squares == 0, math.pi / SCREENING**2, shaped) * (1.0 / N**3)).astype(np.float32)


def point(n1, n2):
    return (5 * n1 + 16 * n2) % N


def frequency(k1, k2):
    k = next(k for k in range(N) if k % 16 == k1 and k % 5 == k2)
    return min(k, N - k)


def turn(re, im, k, n, sign):
    if k == 0:
        return re, im
    if 4 * k == n:
        return (-im, re) if sign > 0 else (im, -re)
    c, s = math.cos(2 * math.pi * k / n), sign * math.sin(2 * math.pi * k / n)
    if 8 * k == n:
        return c * (re - sign * im), c * (im + sign * re)
    if 8 * k == 3 * n:
        return c * (re + sign * im), c * (im - sign * re)
    return c * re - s * im, c * im + s * re


def real_transform(x):
    n = len(x)
    if n == 2:
        return [(x[0] + x[1], None), (x[0] - x[1], None)]
    even, odd = real_transform(x[0::2]), real_transform(x[1::2])
    out = [None] * (n // 2 + 1)
    out[0] = (even[0][0] + odd[0][0], None)
    out[n // 2] = (even[0][0] - odd[0][0], None)
    out[n // 4] = (even[n // 4][0], -odd[n // 4][0])
    for k in range(1, n // 4):
        re, im = turn(*odd[k], k, n, -1)
        out[k] = (even[k][0] + re, even[k][1] + im)
        out[n // 2 - k] = (even[k][0] - re, im - even[k][1])
    return out


def real_inverse(spectrum):
    n = 2 * (len(spectrum) - 1)
    if n == 2:
        return [spectrum[0][0] + spectrum[1][0], spectrum[0][0] - spectrum[1][0]]
    even, odd = [None] * (n // 4 + 1), [None] * (n // 4 + 1)
    even[0] = (spectrum[0][0] + spectrum[n // 2][0], None)
    odd[0] = (spectrum[0][0] - spectrum[n // 2][0], None)
    even[n // 4] = (2.0 * spectrum[n // 4][0], None)
    odd[n // 4] = (-2.0 * spectrum[n // 4][1], None)
    for k in range(1, n // 4):
        (re, im), (re_far, im_far) = spectrum[k], spectrum[n // 2 - k]
        even[k] = (re + re_far, im - im_far)
        odd[k] = turn(re - re_far, im + im_far, k, n, 1)
    out = [None] * n
    out[0::2], out[1::2] = real_inverse(even), real_inverse(odd)
    return out


C1, C2 = math.cos(2 * math.pi / 5), math.cos(4 * math.pi / 5)
S1, S2 = math.sin(2 * math.pi / 5), math.sin(4 * math.pi / 5)


def five_parts(x):
    t1, t2, t3, t4 = x[1] + x[4], x[2] + x[3], x[1] - x[4], x[2] - x[3]
    return (
        x[0] + t1 + t2,
        x[0] + C1 * t1 + C2 * t2,
        x[0] + C2 * t1 + C1 * t2,
        S1 * t3 + S2 * t4,
        S2 * t3 - S1 * t4,
    )


def five_real(x, kernel):
    zero, a1, a2, b1, b2 = five_parts(x)
    zero, a1, a2, b1, b2 = kernel[0] * zero, 2.0 * kernel[1] * a1, 2.0 * kernel[2] * a2, 2.0 * kernel[1] * b1, 2.0 * kernel[2] * b2
    m1, m2 = zero + C1 * a1 + C2 * a2, zero + C2 * a1 + C1 * a2
    n1, n2 = S1 * b1 + S2 * b2, S2 * b1 - S1 * b2
    return [zero + a1 + a2, m1 + n1, m2 + n2, m2 - n2, m1 - n1]


def five_complex(re, im, kernel):
    r0, ra1, ra2, rb1, rb2 = five_parts(re)
    i0, ia1, ia2, ib1, ib2 = five_parts(im)
    r = [kernel[0] * r0, kernel[1] * (ra1 + ib1), kernel[2] * (ra2 + ib2), kernel[3] * (ra2 - ib2), kernel[4] * (ra1 - ib1)]
    i = [kernel[0] * i0, kernel[1] * (ia1 - rb1), kernel[2] * (ia2 - rb2), kernel[3] * (ia2 + rb2), kernel[4] * (ia1 + rb1)]
    r0, ra1, ra2, rb1, rb2 = five_parts(r)
    i0, ia1, ia2, ib1, ib2 = five_parts(i)
    return (
        [r0, ra1 - ib1, ra2 - ib2, ra2 + ib2, ra1 + ib1],
        [i0, ia1 + rb1, ia2 + rb2, ia2 - rb2, ia1 - rb1],
    )


def times(table, data):
    high = data.astype(BF16)
    low = (data - high.astype(F32)).astype(BF16)
    stacked = jnp.concatenate([high, low, high], axis=0)
    return lax.dot_general(table, stacked, (((1,), (0,)), ((), ())), preferred_element_type=F32)


def piece(data, index):
    return data[:, LANES * index : LANES * (index + 1)]


def forwards(table_y, table_to, there, turned):
    fill = jnp.zeros((LANES - N, LANES), F32)

    def forward_y(a, b, first, group):
        start = group * PLANES
        density = jnp.concatenate([a[start + i] * b[start + i] for i in range(PLANES)], axis=1)
        along_y = times(table_y[...], density)
        for i in range(PLANES):
            turned[first + start + i] = jnp.concatenate([piece(along_y, i), fill], axis=0).T

    def forward_z(group):
        start = group * PLANES
        rows = [
            jnp.concatenate(
                [
                    turned[start + j // 2, LOW * (j % 2) : LOW * (j % 2) + LOW],
                    turned[start + 4, HIGH * j : HIGH * (j + 1)],
                ],
                axis=0,
            )
            for j in range(GROUP)
        ]
        along_z = times(table_to[...], jnp.concatenate(rows, axis=1))
        for j in range(GROUP):
            there[group * GROUP + j] = piece(along_z, j)

    return forward_y, forward_z


def unit_body(ready, near_a, near_b, far_a, far_b, table_y, table_to, table_from, kernel, total, out, done, there, back, mid, turned):
    done[0, 0] = 0
    forward_y, forward_z = forwards(table_y, table_to, there, turned)

    def plane_at(x):
        return (there if ready is None or x >= HALF else ready).at[x]

    def middle(group, kernel_group):
        rows = pl.ds(pl.multiple_of(group * GROUP, GROUP), GROUP)
        for n2 in range(5):
            for k1, (re, im) in enumerate(real_transform([plane_at(point(n1, n2))[rows, :] for n1 in range(16)])):
                mid[2 * k1, n2] = re
                if im is not None:
                    mid[2 * k1 + 1, n2] = im
        for k1 in range(9):
            scale = [kernel[kernel_group, frequency(k1, k2)] for k2 in range(5)]
            re = [mid[2 * k1, n2] for n2 in range(5)]
            if k1 in (0, 8):
                re = five_real(re, scale)
            else:
                re, im = five_complex(re, [mid[2 * k1 + 1, n2] for n2 in range(5)], scale)
                for n2 in range(5):
                    mid[2 * k1 + 1, n2] = im[n2]
            for n2 in range(5):
                mid[2 * k1, n2] = re[n2]
        for n2 in range(5):
            spectrum = [(mid[2 * k1, n2], None if k1 in (0, 8) else mid[2 * k1 + 1, n2]) for k1 in range(9)]
            for n1, value in enumerate(real_inverse(spectrum)):
                if point(n1, n2) < HALF:
                    back[point(n1, n2), rows, :] = value

    def backward_z(group):
        rows = [back[group * GROUP + j] for j in range(GROUP)]
        along_z = times(table_from[...], jnp.concatenate(rows, axis=1))
        parts = [piece(along_z, j) for j in range(GROUP)]
        packed = [jnp.concatenate([parts[2 * i][:LOW], parts[2 * i + 1][:LOW]], axis=0) for i in range(4)]
        packed.append(jnp.concatenate([part[LOW:] for part in parts], axis=0))
        for i, plane in enumerate(packed):
            turned[group * PLANES + i] = plane.T

    def backward_y(group):
        start = group * PLANES
        planes = jnp.concatenate([turned[start + i, :N] for i in range(PLANES)], axis=1)
        potential = times(table_y[...], planes)
        for i in range(PLANES):
            term = piece(potential, i) * near_b[start + i]
            out[start + i] = term if total is None else total[start + i] + term

    for group in range(GROUPS):
        if ready is None:
            forward_y(near_a, near_b, 0, group)
        forward_y(far_a, far_b, GROUPS * PLANES, group)
    for group in range(0 if ready is None else GROUPS, 2 * GROUPS):
        forward_z(group)

    @pl.loop(0, 2 * GROUPS)
    def _(group):
        middle(group, jnp.where(group > GROUPS, group - GROUPS, group))

    for group in range(GROUPS):
        backward_z(group)
    for group in range(GROUPS):
        backward_y(group)


def unit(a, b, constants, after, total=None, waits=(), near_at=None, ready=None):
    operands = [a[0], b[0], a[1], b[1], *constants]

    def body(order, *refs):
        refs = list(refs[len(waits) :])
        near_ready = None if ready is None else refs.pop(0)
        if near_at is not None:
            sent = refs.pop(len(operands) + (total is not None) + 2)
            copy_chosen(near_at, refs[0], refs[2], sent)
        ins, rest = refs[: len(operands)], refs[len(operands) :]
        if total is None:
            unit_body(near_ready, *ins, None, *rest)
        else:
            unit_body(near_ready, *ins, *rest)

    here = pl.BlockSpec(memory_space=pltpu.VMEM)
    scalar = pl.BlockSpec(memory_space=pltpu.SMEM)
    operands_all = (*(() if ready is None else (ready,)), *operands, *(() if total is None else (total,)))
    return pl.pallas_call(
        body,
        in_specs=[scalar] + [pl.BlockSpec(memory_space=pl.ANY)] * len(waits) + [here] * len(operands_all),
        out_specs=(here, scalar) + (here,) * (near_at is not None),
        out_shape=(jax.ShapeDtypeStruct(PACKED, F32), jax.ShapeDtypeStruct((1, 1), jnp.int32))
        + (jax.ShapeDtypeStruct(PACKED, F32),) * (near_at is not None),
        scratch_shapes=[
            pltpu.VMEM((N, N, LANES), F32),
            pltpu.VMEM((HALF, N, LANES), F32),
            pltpu.VMEM((17, 5, GROUP, LANES), F32),
            pltpu.VMEM((2 * GROUPS * PLANES, LANES, LANES), F32),
        ],
        compiler_params=pltpu.CompilerParams(vmem_limit_bytes=20 * 2**20),
        cost_estimate=pl.CostEstimate(flops=1, bytes_accessed=1, transcendentals=0),
        name="unit",
    )(after, *waits, *operands_all)


def ahead_body(a, a_2, b, table_y, table_to, out, out_2, turned, turned_2):
    steps = [forwards(table_y, table_to, out, turned), forwards(table_y, table_to, out_2, turned_2)]
    for group in range(GROUPS):
        steps[0][0](a, b, 0, group)
        steps[1][0](a_2, b, 0, group)
    for group in range(GROUPS):
        steps[0][1](group)
        steps[1][1](group)


def ahead(a, a_2, b, constants):
    here = pl.BlockSpec(memory_space=pltpu.VMEM)
    return pl.pallas_call(
        ahead_body,
        in_specs=[here] * 5,
        out_specs=(here, here),
        out_shape=(jax.ShapeDtypeStruct((HALF, N, LANES), F32),) * 2,
        scratch_shapes=[pltpu.VMEM((GROUPS * PLANES, LANES, LANES), F32)] * 2,
        compiler_params=pltpu.CompilerParams(vmem_limit_bytes=16 * 2**20),
        cost_estimate=pl.CostEstimate(flops=1, bytes_accessed=1, transcendentals=0),
        name="ahead",
    )(a, a_2, b, constants[0], constants[1])


def copy_chosen(places, a, b, out):
    place = lax.axis_index("band")
    takes = functools.reduce(jnp.logical_or, [place == p for p in places])

    @pl.when(takes)
    def _():
        @pl.loop(0, GROUPS * PLANES)
        def _(plane):
            out[plane] = a[plane]

    @pl.when(jnp.logical_not(takes))
    def _():
        @pl.loop(0, GROUPS * PLANES)
        def _(plane):
            out[plane] = b[plane]


def choose_body(places, order, a, b, out):
    copy_chosen(places, a, b, out)


def choose(places, a, b, after):
    here = pl.BlockSpec(memory_space=pltpu.VMEM)
    return pl.pallas_call(
        functools.partial(choose_body, places),
        in_specs=[pl.BlockSpec(memory_space=pltpu.SMEM), here, here],
        out_specs=here,
        out_shape=jax.ShapeDtypeStruct(PACKED, F32),
        compiler_params=pltpu.CompilerParams(vmem_limit_bytes=8 * 2**20),
        cost_estimate=pl.CostEstimate(flops=1, bytes_accessed=1, transcendentals=0),
        name="choose",
    )(after, a, b)


def pack_body(data, out):
    lane = lax.broadcasted_iota(jnp.int32, (N, LANES), 1)
    pad = jnp.zeros((N, LANES - N), F32)

    @pl.loop(0, GROUPS)
    def _(group):
        last = None
        for i in range(4):
            pair = [jnp.concatenate([data[group * GROUP + 2 * i + h], pad], axis=1) for h in range(2)]
            out[group * PLANES + i] = jnp.where(lane < LOW, pair[0], pltpu.roll(pair[1], LOW, 1))
            for h in range(2):
                place = HIGH * (2 * i + h)
                moved = pltpu.roll(pair[h], (place - LOW) % LANES, 1) if place != LOW else pair[h]
                last = moved if last is None else jnp.where(lane >= place, moved, last)
        out[group * PLANES + 4] = last


def pack(data):
    return pl.pallas_call(
        pack_body,
        out_shape=jax.ShapeDtypeStruct(PACKED, F32),
        compiler_params=pltpu.CompilerParams(vmem_limit_bytes=16 * 2**20),
        name="pack",
    )(data)


def unpack_body(total, returned, theirs, out, held, sems):
    lane = lax.broadcasted_iota(jnp.int32, (N, LANES), 1)
    copies = []
    for group in range(GROUPS):
        start = group * PLANES
        planes = [total[start + i] + returned[start + i] + theirs[start + i] for i in range(PLANES)]
        for j in range(GROUP):
            low = planes[j // 2] if j % 2 == 0 else pltpu.roll(planes[j // 2], LOW, 1)
            place = HIGH * j
            high = pltpu.roll(planes[4], (LOW - place) % LANES, 1) if place != LOW else planes[4]
            held[group, j] = jnp.where(lane < LOW, low, high)[:, :N]
        copies.append(pltpu.make_async_copy(held.at[group], out.at[pl.ds(group * GROUP, GROUP)], sems.at[group]))
        copies[-1].start()
    for copy in copies:
        copy.wait()


def unpack_sum(total, returned, theirs):
    return pl.pallas_call(
        unpack_body,
        in_specs=[pl.BlockSpec(memory_space=pltpu.VMEM)] * 3,
        out_specs=pl.BlockSpec(memory_space=pltpu.HBM),
        out_shape=jax.ShapeDtypeStruct((HALF, N, N), F32),
        scratch_shapes=[pltpu.VMEM((GROUPS, GROUP, N, N), F32), pltpu.SemaphoreType.DMA((GROUPS,))],
        compiler_params=pltpu.CompilerParams(vmem_limit_bytes=16 * 2**20),
        name="unpack_sum",
    )(total, returned, theirs)


def shards(orbitals):
    bands = lax.axis_size("band")
    half = bands // 2
    sides = [1 if b % 2 else -1 for b in range(bands)]

    def sources(distance):
        return [(b + distance * sides[b]) % bands for b in range(bands)]

    def takers(distance):
        return [b for b, source in enumerate(sources(distance)) if b // half != source // half]

    def from_place(data, distance):
        return lax.ppermute(data, "band", [(source, b) for b, source in enumerate(sources(distance))])

    def from_half(data, distance):
        return lax.ppermute(data, "band", [(b // half * half + source % half, b) for b, source in enumerate(sources(distance))])

    def far_route(distance):
        route = []
        for b, source in enumerate(sources(distance)):
            for slab in range(2):
                route.append((2 * source + (1 - slab if b in takers(distance) else slab), 2 * b + slab))
        return route

    def swapped_halves(data, distance):
        return lax.ppermute(data, "band", [((b + half) % bands, b) for b in takers(distance)])

    def givers(distance):
        return [sources(distance)[b] for b in takers(distance)]

    def other_core(data):
        return from_place(data, -1)

    constants = tuple(jnp.asarray(t) for t in (*tables(), screened_kernel()))
    near = pack(orbitals[0])
    far = lax.ppermute(near, "grid", [(0, 1), (1, 0)])
    m2_half = from_half(near, -2)
    p2_half = from_half(near, 2)
    far, m2_half, p2_half = lax.optimization_barrier((far, m2_half, p2_half))
    own = (near, far)
    first = jnp.zeros((1, 1), jnp.int32)
    m2_far = lax.ppermute(choose(givers(-2), near, far, first), ("band", "grid"), far_route(-2))
    m1 = (other_core(near), other_core(far))
    m2_swapped = swapped_halves(m2_half, -2)
    total, after, p2_sent = unit(own, m1, constants, first, near_at=givers(2))
    p2_far = lax.ppermute(p2_sent, ("band", "grid"), far_route(2))
    p2_half, after = lax.optimization_barrier((p2_half, after))
    p2_swapped = swapped_halves(p2_half, 2)
    m2_near = choose(takers(-2), m2_swapped, m2_half, after)
    p1_near = other_core(m2_near)
    own_m2, m1_m2 = ahead(near, m1[0], m2_near, constants)
    m2_far, p1_near, own_m2, m1_m2, after = lax.optimization_barrier((m2_far, p1_near, own_m2, m1_m2, after))
    m2 = (m2_near, m2_far)
    p1 = (p1_near, other_core(m2_far))
    total, after = unit(own, m2, constants, after, total, ready=own_m2)
    lent, after = unit(m2, p1, constants, after)
    returned = from_place(lent, 2)
    partner, after = unit(m1, m2, constants, after, waits=(p2_far,), ready=m1_m2)
    p2 = (choose(takers(2), p2_swapped, p2_half, after), p2_far)
    partner, after = unit(m1, p2, constants, after, partner)
    theirs = other_core(partner)
    total, after = unit(own, p2, constants, after, total, waits=(returned,))
    return unpack_sum(total, returned, theirs)[None]


def solution(mesh):
    spec = P("band", "grid", None, None)
    return jax.shard_map(shards, mesh=mesh, in_specs=(spec,), out_specs=spec, check_vma=False)
```

```python
import functools
import math

import jax
import jax.numpy as jnp
import numpy as np
from jax import lax
from jax.experimental import pallas as pl
from jax.experimental.pallas import tpu as pltpu
from jax.sharding import PartitionSpec as P

CELL_LENGTH = 37.2
SCREENING = 0.106
BF16 = jnp.bfloat16
F32 = jnp.float32
N = 80
HALF = N // 2
GROUP = 8
GROUPS = HALF // GROUP
PLANES = 5
PACKED = (GROUPS * PLANES, N, 128)
LANES = 128
LOW, HIGH = 64, 16

FOLD = np.concatenate([np.arange(HALF), [HALF], np.arange(N - 1, HALF, -1)])


def cas(rows, columns):
    angles = (rows[:, None] * columns[None, :] % N) * (2.0 * math.pi / N)
    return np.cos(angles) + np.sin(angles)


def three_terms(table):
    high = table.astype(np.float32).astype(jnp.bfloat16)
    low = (table - high.astype(np.float64)).astype(np.float32).astype(jnp.bfloat16)
    return np.concatenate([high, high, low], axis=1)


def tables():
    places = np.arange(N)
    return (
        three_terms(cas(places, places)),
        three_terms(cas(FOLD, places)),
        three_terms(cas(places, FOLD)),
    )


def screened_kernel():
    line = np.arange(N)
    freq_y = np.pad(np.where(2 * line >= N, line - N, line), (0, LANES - N))[None, None, None, :]
    freq_x = np.arange(HALF + 1)[None, :, None, None]
    freq_z = np.concatenate([np.arange(HALF + 1), np.arange(1, GROUP)]).reshape(6, 1, GROUP, 1)
    squares = freq_x * freq_x + freq_y * freq_y + freq_z * freq_z
    wave_square = np.where(squares == 0, 1, squares) * (2.0 * math.pi / CELL_LENGTH) ** 2
    shaped = 4.0 * math.pi / wave_square * (1.0 - np.exp(-wave_square / (4.0 * SCREENING**2)))
    return (np.where(squares == 0, math.pi / SCREENING**2, shaped) * (1.0 / N**3)).astype(np.float32)


def point(n1, n2):
    return (5 * n1 + 16 * n2) % N


def frequency(k1, k2):
    k = next(k for k in range(N) if k % 16 == k1 and k % 5 == k2)
    return min(k, N - k)


def turn(re, im, k, n, sign):
    if k == 0:
        return re, im
    if 4 * k == n:
        return (-im, re) if sign > 0 else (im, -re)
    c, s = math.cos(2 * math.pi * k / n), sign * math.sin(2 * math.pi * k / n)
    if 8 * k == n:
        return c * (re - sign * im), c * (im + sign * re)
    if 8 * k == 3 * n:
        return c * (re + sign * im), c * (im - sign * re)
    return c * re - s * im, c * im + s * re


def real_transform(x):
    n = len(x)
    if n == 2:
        return [(x[0] + x[1], None), (x[0] - x[1], None)]
    even, odd = real_transform(x[0::2]), real_transform(x[1::2])
    out = [None] * (n // 2 + 1)
    out[0] = (even[0][0] + odd[0][0], None)
    out[n // 2] = (even[0][0] - odd[0][0], None)
    out[n // 4] = (even[n // 4][0], -odd[n // 4][0])
    for k in range(1, n // 4):
        re, im = turn(*odd[k], k, n, -1)
        out[k] = (even[k][0] + re, even[k][1] + im)
        out[n // 2 - k] = (even[k][0] - re, im - even[k][1])
    return out


def real_inverse(spectrum):
    n = 2 * (len(spectrum) - 1)
    if n == 2:
        return [spectrum[0][0] + spectrum[1][0], spectrum[0][0] - spectrum[1][0]]
    even, odd = [None] * (n // 4 + 1), [None] * (n // 4 + 1)
    even[0] = (spectrum[0][0] + spectrum[n // 2][0], None)
    odd[0] = (spectrum[0][0] - spectrum[n // 2][0], None)
    even[n // 4] = (2.0 * spectrum[n // 4][0], None)
    odd[n // 4] = (-2.0 * spectrum[n // 4][1], None)
    for k in range(1, n // 4):
        (re, im), (re_far, im_far) = spectrum[k], spectrum[n // 2 - k]
        even[k] = (re + re_far, im - im_far)
        odd[k] = turn(re - re_far, im + im_far, k, n, 1)
    out = [None] * n
    out[0::2], out[1::2] = real_inverse(even), real_inverse(odd)
    return out


C1, C2 = math.cos(2 * math.pi / 5), math.cos(4 * math.pi / 5)
S1, S2 = math.sin(2 * math.pi / 5), math.sin(4 * math.pi / 5)


def five_parts(x):
    t1, t2, t3, t4 = x[1] + x[4], x[2] + x[3], x[1] - x[4], x[2] - x[3]
    return (
        x[0] + t1 + t2,
        x[0] + C1 * t1 + C2 * t2,
        x[0] + C2 * t1 + C1 * t2,
        S1 * t3 + S2 * t4,
        S2 * t3 - S1 * t4,
    )


def five_real(x, kernel):
    zero, a1, a2, b1, b2 = five_parts(x)
    zero, a1, a2, b1, b2 = kernel[0] * zero, 2.0 * kernel[1] * a1, 2.0 * kernel[2] * a2, 2.0 * kernel[1] * b1, 2.0 * kernel[2] * b2
    m1, m2 = zero + C1 * a1 + C2 * a2, zero + C2 * a1 + C1 * a2
    n1, n2 = S1 * b1 + S2 * b2, S2 * b1 - S1 * b2
    return [zero + a1 + a2, m1 + n1, m2 + n2, m2 - n2, m1 - n1]


def five_complex(re, im, kernel):
    r0, ra1, ra2, rb1, rb2 = five_parts(re)
    i0, ia1, ia2, ib1, ib2 = five_parts(im)
    r = [kernel[0] * r0, kernel[1] * (ra1 + ib1), kernel[2] * (ra2 + ib2), kernel[3] * (ra2 - ib2), kernel[4] * (ra1 - ib1)]
    i = [kernel[0] * i0, kernel[1] * (ia1 - rb1), kernel[2] * (ia2 - rb2), kernel[3] * (ia2 + rb2), kernel[4] * (ia1 + rb1)]
    r0, ra1, ra2, rb1, rb2 = five_parts(r)
    i0, ia1, ia2, ib1, ib2 = five_parts(i)
    return (
        [r0, ra1 - ib1, ra2 - ib2, ra2 + ib2, ra1 + ib1],
        [i0, ia1 + rb1, ia2 + rb2, ia2 - rb2, ia1 - rb1],
    )


def times(table, data):
    high = data.astype(BF16)
    low = (data - high.astype(F32)).astype(BF16)
    stacked = jnp.concatenate([high, low, high], axis=0)
    return lax.dot_general(table, stacked, (((1,), (0,)), ((), ())), preferred_element_type=F32)


def piece(data, index):
    return data[:, LANES * index : LANES * (index + 1)]


def forwards(table_y, table_to, there, turned):
    fill = jnp.zeros((LANES - N, LANES), F32)

    def forward_y(a, b, first, group):
        start = group * PLANES
        density = jnp.concatenate([a[start + i] * b[start + i] for i in range(PLANES)], axis=1)
        along_y = times(table_y[...], density)
        for i in range(PLANES):
            turned[first + start + i] = jnp.concatenate([piece(along_y, i), fill], axis=0).T

    def forward_z(group):
        start = group * PLANES
        rows = [
            jnp.concatenate(
                [
                    turned[start + j // 2, LOW * (j % 2) : LOW * (j % 2) + LOW],
                    turned[start + 4, HIGH * j : HIGH * (j + 1)],
                ],
                axis=0,
            )
            for j in range(GROUP)
        ]
        along_z = times(table_to[...], jnp.concatenate(rows, axis=1))
        for j in range(GROUP):
            there[group * GROUP + j] = piece(along_z, j)

    return forward_y, forward_z


def unit_body(ready, near_a, near_b, far_a, far_b, table_y, table_to, table_from, kernel, total, out, done, there, back, mid, turned):
    done[0, 0] = 0
    forward_y, forward_z = forwards(table_y, table_to, there, turned)

    def plane_at(x):
        return (there if ready is None or x >= HALF else ready).at[x]

    def middle(group, kernel_group):
        rows = pl.ds(pl.multiple_of(group * GROUP, GROUP), GROUP)
        for n2 in range(5):
            for k1, (re, im) in enumerate(real_transform([plane_at(point(n1, n2))[rows, :] for n1 in range(16)])):
                mid[2 * k1, n2] = re
                if im is not None:
                    mid[2 * k1 + 1, n2] = im
        for k1 in range(9):
            scale = [kernel[kernel_group, frequency(k1, k2)] for k2 in range(5)]
            re = [mid[2 * k1, n2] for n2 in range(5)]
            if k1 in (0, 8):
                re = five_real(re, scale)
            else:
                re, im = five_complex(re, [mid[2 * k1 + 1, n2] for n2 in range(5)], scale)
                for n2 in range(5):
                    mid[2 * k1 + 1, n2] = im[n2]
            for n2 in range(5):
                mid[2 * k1, n2] = re[n2]
        for n2 in range(5):
            spectrum = [(mid[2 * k1, n2], None if k1 in (0, 8) else mid[2 * k1 + 1, n2]) for k1 in range(9)]
            for n1, value in enumerate(real_inverse(spectrum)):
                if point(n1, n2) < HALF:
                    back[point(n1, n2), rows, :] = value

    def backward_z(group):
        rows = [back[group * GROUP + j] for j in range(GROUP)]
        along_z = times(table_from[...], jnp.concatenate(rows, axis=1))
        parts = [piece(along_z, j) for j in range(GROUP)]
        packed = [jnp.concatenate([parts[2 * i][:LOW], parts[2 * i + 1][:LOW]], axis=0) for i in range(4)]
        packed.append(jnp.concatenate([part[LOW:] for part in parts], axis=0))
        for i, plane in enumerate(packed):
            turned[group * PLANES + i] = plane.T

    def backward_y(group):
        start = group * PLANES
        planes = jnp.concatenate([turned[start + i, :N] for i in range(PLANES)], axis=1)
        potential = times(table_y[...], planes)
        for i in range(PLANES):
            term = piece(potential, i) * near_b[start + i]
            out[start + i] = term if total is None else total[start + i] + term

    for group in range(GROUPS):
        if ready is None:
            forward_y(near_a, near_b, 0, group)
        forward_y(far_a, far_b, GROUPS * PLANES, group)
    for group in range(0 if ready is None else GROUPS, 2 * GROUPS):
        forward_z(group)

    @pl.loop(0, 2 * GROUPS)
    def _(group):
        middle(group, jnp.where(group > GROUPS, group - GROUPS, group))

    for group in range(GROUPS):
        backward_z(group)
    for group in range(GROUPS):
        backward_y(group)


def unit(a, b, constants, after, total=None, waits=(), pick=None, ready=None):
    operands = [a[0], b[0], a[1], b[1], *constants]

    def body(order, *refs):
        refs = list(refs[len(waits) :])
        near_ready = None if ready is None else refs.pop(0)
        if pick is not None:
            x, y, picked = refs.pop(0), refs.pop(0), refs.pop(len(operands) + (total is not None) + 2)
            copy_chosen(pick[0], x, y, picked)
        ins, rest = refs[: len(operands)], refs[len(operands) :]
        if total is None:
            unit_body(near_ready, *ins, None, *rest)
        else:
            unit_body(near_ready, *ins, *rest)

    here = pl.BlockSpec(memory_space=pltpu.VMEM)
    scalar = pl.BlockSpec(memory_space=pltpu.SMEM)
    operands_all = (*(() if ready is None else (ready,)), *(() if pick is None else pick[1:]), *operands, *(() if total is None else (total,)))
    return pl.pallas_call(
        body,
        in_specs=[scalar] + [pl.BlockSpec(memory_space=pl.ANY)] * len(waits) + [here] * len(operands_all),
        out_specs=(here, scalar) + (here,) * (pick is not None),
        out_shape=(jax.ShapeDtypeStruct(PACKED, F32), jax.ShapeDtypeStruct((1, 1), jnp.int32))
        + (jax.ShapeDtypeStruct(PACKED, F32),) * (pick is not None),
        scratch_shapes=[
            pltpu.VMEM((N, N, LANES), F32),
            pltpu.VMEM((HALF, N, LANES), F32),
            pltpu.VMEM((17, 5, GROUP, LANES), F32),
            pltpu.VMEM((2 * GROUPS * PLANES, LANES, LANES), F32),
        ],
        compiler_params=pltpu.CompilerParams(vmem_limit_bytes=20 * 2**20),
        cost_estimate=pl.CostEstimate(flops=1, bytes_accessed=1, transcendentals=0),
        name="unit",
    )(after, *waits, *operands_all)


def ahead_body(a, a_2, b, table_y, table_to, out, out_2, turned, turned_2):
    steps = [forwards(table_y, table_to, out, turned), forwards(table_y, table_to, out_2, turned_2)]
    for group in range(GROUPS):
        steps[0][0](a, b, 0, group)
        steps[1][0](a_2, b, 0, group)
    for group in range(GROUPS):
        steps[0][1](group)
        steps[1][1](group)


def ahead(a, a_2, b, constants):
    here = pl.BlockSpec(memory_space=pltpu.VMEM)
    return pl.pallas_call(
        ahead_body,
        in_specs=[here] * 5,
        out_specs=(here, here),
        out_shape=(jax.ShapeDtypeStruct((HALF, N, LANES), F32),) * 2,
        scratch_shapes=[pltpu.VMEM((GROUPS * PLANES, LANES, LANES), F32)] * 2,
        compiler_params=pltpu.CompilerParams(vmem_limit_bytes=16 * 2**20),
        cost_estimate=pl.CostEstimate(flops=1, bytes_accessed=1, transcendentals=0),
        name="ahead",
    )(a, a_2, b, constants[0], constants[1])


def copy_chosen(places, a, b, out):
    place = lax.axis_index("band")
    takes = functools.reduce(jnp.logical_or, [place == p for p in places])

    @pl.when(takes)
    def _():
        @pl.loop(0, GROUPS * PLANES)
        def _(plane):
            out[plane] = a[plane]

    @pl.when(jnp.logical_not(takes))
    def _():
        @pl.loop(0, GROUPS * PLANES)
        def _(plane):
            out[plane] = b[plane]


def choose_body(places, order, a, b, out):
    copy_chosen(places, a, b, out)


def choose(places, a, b, after):
    here = pl.BlockSpec(memory_space=pltpu.VMEM)
    return pl.pallas_call(
        functools.partial(choose_body, places),
        in_specs=[pl.BlockSpec(memory_space=pltpu.SMEM), here, here],
        out_specs=here,
        out_shape=jax.ShapeDtypeStruct(PACKED, F32),
        compiler_params=pltpu.CompilerParams(vmem_limit_bytes=8 * 2**20),
        cost_estimate=pl.CostEstimate(flops=1, bytes_accessed=1, transcendentals=0),
        name="choose",
    )(after, a, b)


def pack_body(data, out):
    lane = lax.broadcasted_iota(jnp.int32, (N, LANES), 1)
    pad = jnp.zeros((N, LANES - N), F32)

    @pl.loop(0, GROUPS)
    def _(group):
        last = None
        for i in range(4):
            pair = [jnp.concatenate([data[group * GROUP + 2 * i + h], pad], axis=1) for h in range(2)]
            out[group * PLANES + i] = jnp.where(lane < LOW, pair[0], pltpu.roll(pair[1], LOW, 1))
            for h in range(2):
                place = HIGH * (2 * i + h)
                moved = pltpu.roll(pair[h], (place - LOW) % LANES, 1) if place != LOW else pair[h]
                last = moved if last is None else jnp.where(lane >= place, moved, last)
        out[group * PLANES + 4] = last


def pack(data):
    return pl.pallas_call(
        pack_body,
        out_shape=jax.ShapeDtypeStruct(PACKED, F32),
        compiler_params=pltpu.CompilerParams(vmem_limit_bytes=16 * 2**20),
        name="pack",
    )(data)


def unpack_body(total, returned, theirs, out, held, sems):
    lane = lax.broadcasted_iota(jnp.int32, (N, LANES), 1)
    copies = []
    for group in range(GROUPS):
        start = group * PLANES
        planes = [total[start + i] + returned[start + i] + theirs[start + i] for i in range(PLANES)]
        for j in range(GROUP):
            low = planes[j // 2] if j % 2 == 0 else pltpu.roll(planes[j // 2], LOW, 1)
            place = HIGH * j
            high = pltpu.roll(planes[4], (LOW - place) % LANES, 1) if place != LOW else planes[4]
            held[group, j] = jnp.where(lane < LOW, low, high)[:, :N]
        copies.append(pltpu.make_async_copy(held.at[group], out.at[pl.ds(group * GROUP, GROUP)], sems.at[group]))
        copies[-1].start()
    for copy in copies:
        copy.wait()


def unpack_sum(total, returned, theirs):
    return pl.pallas_call(
        unpack_body,
        in_specs=[pl.BlockSpec(memory_space=pltpu.VMEM)] * 3,
        out_specs=pl.BlockSpec(memory_space=pltpu.HBM),
        out_shape=jax.ShapeDtypeStruct((HALF, N, N), F32),
        scratch_shapes=[pltpu.VMEM((GROUPS, GROUP, N, N), F32), pltpu.SemaphoreType.DMA((GROUPS,))],
        compiler_params=pltpu.CompilerParams(vmem_limit_bytes=16 * 2**20),
        name="unpack_sum",
    )(total, returned, theirs)


def shards(orbitals):
    bands = lax.axis_size("band")
    half = bands // 2
    sides = [1 if b % 2 else -1 for b in range(bands)]

    def sources(distance):
        return [(b + distance * sides[b]) % bands for b in range(bands)]

    def takers(distance):
        return [b for b, source in enumerate(sources(distance)) if b // half != source // half]

    def from_place(data, distance):
        return lax.ppermute(data, "band", [(source, b) for b, source in enumerate(sources(distance))])

    def from_half(data, distance):
        return lax.ppermute(data, "band", [(b // half * half + source % half, b) for b, source in enumerate(sources(distance))])

    def far_route(distance):
        route = []
        for b, source in enumerate(sources(distance)):
            for slab in range(2):
                route.append((2 * source + (1 - slab if b in takers(distance) else slab), 2 * b + slab))
        return route

    def swapped_halves(data, distance):
        return lax.ppermute(data, "band", [((b + half) % bands, b) for b in takers(distance)])

    def givers(distance):
        return [sources(distance)[b] for b in takers(distance)]

    def other_core(data):
        return from_place(data, -1)

    constants = tuple(jnp.asarray(t) for t in (*tables(), screened_kernel()))
    near = pack(orbitals[0])
    far = lax.ppermute(near, "grid", [(0, 1), (1, 0)])
    m2_half = from_half(near, -2)
    p2_half = from_half(near, 2)
    far, m2_half, p2_half = lax.optimization_barrier((far, m2_half, p2_half))
    own = (near, far)
    first = jnp.zeros((1, 1), jnp.int32)
    m2_far = lax.ppermute(choose(givers(-2), near, far, first), ("band", "grid"), far_route(-2))
    m1 = (other_core(near), other_core(far))
    m2_swapped = swapped_halves(m2_half, -2)
    total, after, p2_sent = unit(own, m1, constants, first, pick=(givers(2), near, far))
    p2_far = lax.ppermute(p2_sent, ("band", "grid"), far_route(2))
    p2_half, after = lax.optimization_barrier((p2_half, after))
    p2_swapped = swapped_halves(p2_half, 2)
    m2_near = choose(takers(-2), m2_swapped, m2_half, after)
    p1_near = other_core(m2_near)
    own_m2, m1_m2 = ahead(near, m1[0], m2_near, constants)
    m2_far, p1_near, own_m2, m1_m2, after = lax.optimization_barrier((m2_far, p1_near, own_m2, m1_m2, after))
    m2 = (m2_near, m2_far)
    p1 = (p1_near, other_core(m2_far))
    total, after = unit(own, m2, constants, after, total, ready=own_m2)
    lent, after = unit(m2, p1, constants, after)
    returned = from_place(lent, 2)
    partner, after, p2_near = unit(
        m1, m2, constants, after, waits=(p2_far,), pick=(takers(2), p2_swapped, p2_half), ready=m1_m2
    )
    p2 = (p2_near, p2_far)
    partner, after = unit(m1, p2, constants, after, partner)
    theirs = other_core(partner)
    total, after = unit(own, p2, constants, after, total, waits=(returned,))
    return unpack_sum(total, returned, theirs)[None]


def solution(mesh):
    spec = P("band", "grid", None, None)
    return jax.shard_map(shards, mesh=mesh, in_specs=(spec,), out_specs=spec, check_vma=False)
```

```python
import functools
import math

import jax
import jax.numpy as jnp
import numpy as np
from jax import lax
from jax.experimental import pallas as pl
from jax.experimental.pallas import tpu as pltpu
from jax.sharding import PartitionSpec as P

CELL_LENGTH = 37.2
SCREENING = 0.106
BF16 = jnp.bfloat16
F32 = jnp.float32
N = 80
HALF = N // 2
GROUP = 8
GROUPS = HALF // GROUP
PLANES = 5
PACKED = (GROUPS * PLANES, N, 128)
LANES = 128
LOW, HIGH = 64, 16

FOLD = np.concatenate([np.arange(HALF), [HALF], np.arange(N - 1, HALF, -1)])


def cas(rows, columns):
    angles = (rows[:, None] * columns[None, :] % N) * (2.0 * math.pi / N)
    return np.cos(angles) + np.sin(angles)


def three_terms(table):
    high = table.astype(np.float32).astype(jnp.bfloat16)
    low = (table - high.astype(np.float64)).astype(np.float32).astype(jnp.bfloat16)
    return np.concatenate([high, high, low], axis=1)


def tables():
    places = np.arange(N)
    return (
        three_terms(cas(places, places)),
        three_terms(cas(FOLD, places)),
        three_terms(cas(places, FOLD)),
    )


def screened_kernel():
    line = np.arange(N)
    freq_y = np.pad(np.where(2 * line >= N, line - N, line), (0, LANES - N))[None, None, None, :]
    freq_x = np.arange(HALF + 1)[None, :, None, None]
    freq_z = np.concatenate([np.arange(HALF + 1), np.arange(1, GROUP)]).reshape(6, 1, GROUP, 1)
    squares = freq_x * freq_x + freq_y * freq_y + freq_z * freq_z
    wave_square = np.where(squares == 0, 1, squares) * (2.0 * math.pi / CELL_LENGTH) ** 2
    shaped = 4.0 * math.pi / wave_square * (1.0 - np.exp(-wave_square / (4.0 * SCREENING**2)))
    return (np.where(squares == 0, math.pi / SCREENING**2, shaped) * (1.0 / N**3)).astype(np.float32)


def point(n1, n2):
    return (5 * n1 + 16 * n2) % N


def frequency(k1, k2):
    k = next(k for k in range(N) if k % 16 == k1 and k % 5 == k2)
    return min(k, N - k)


def turn(re, im, k, n, sign):
    if k == 0:
        return re, im
    if 4 * k == n:
        return (-im, re) if sign > 0 else (im, -re)
    c, s = math.cos(2 * math.pi * k / n), sign * math.sin(2 * math.pi * k / n)
    if 8 * k == n:
        return c * (re - sign * im), c * (im + sign * re)
    if 8 * k == 3 * n:
        return c * (re + sign * im), c * (im - sign * re)
    return c * re - s * im, c * im + s * re


def real_transform(x):
    n = len(x)
    if n == 2:
        return [(x[0] + x[1], None), (x[0] - x[1], None)]
    even, odd = real_transform(x[0::2]), real_transform(x[1::2])
    out = [None] * (n // 2 + 1)
    out[0] = (even[0][0] + odd[0][0], None)
    out[n // 2] = (even[0][0] - odd[0][0], None)
    out[n // 4] = (even[n // 4][0], -odd[n // 4][0])
    for k in range(1, n // 4):
        re, im = turn(*odd[k], k, n, -1)
        out[k] = (even[k][0] + re, even[k][1] + im)
        out[n // 2 - k] = (even[k][0] - re, im - even[k][1])
    return out


def real_inverse(spectrum):
    n = 2 * (len(spectrum) - 1)
    if n == 2:
        return [spectrum[0][0] + spectrum[1][0], spectrum[0][0] - spectrum[1][0]]
    even, odd = [None] * (n // 4 + 1), [None] * (n // 4 + 1)
    even[0] = (spectrum[0][0] + spectrum[n // 2][0], None)
    odd[0] = (spectrum[0][0] - spectrum[n // 2][0], None)
    even[n // 4] = (2.0 * spectrum[n // 4][0], None)
    odd[n // 4] = (-2.0 * spectrum[n // 4][1], None)
    for k in range(1, n // 4):
        (re, im), (re_far, im_far) = spectrum[k], spectrum[n // 2 - k]
        even[k] = (re + re_far, im - im_far)
        odd[k] = turn(re - re_far, im + im_far, k, n, 1)
    out = [None] * n
    out[0::2], out[1::2] = real_inverse(even), real_inverse(odd)
    return out


C1, C2 = math.cos(2 * math.pi / 5), math.cos(4 * math.pi / 5)
S1, S2 = math.sin(2 * math.pi / 5), math.sin(4 * math.pi / 5)


def five_parts(x):
    t1, t2, t3, t4 = x[1] + x[4], x[2] + x[3], x[1] - x[4], x[2] - x[3]
    return (
        x[0] + t1 + t2,
        x[0] + C1 * t1 + C2 * t2,
        x[0] + C2 * t1 + C1 * t2,
        S1 * t3 + S2 * t4,
        S2 * t3 - S1 * t4,
    )


def five_real(x, kernel):
    zero, a1, a2, b1, b2 = five_parts(x)
    zero, a1, a2, b1, b2 = kernel[0] * zero, 2.0 * kernel[1] * a1, 2.0 * kernel[2] * a2, 2.0 * kernel[1] * b1, 2.0 * kernel[2] * b2
    m1, m2 = zero + C1 * a1 + C2 * a2, zero + C2 * a1 + C1 * a2
    n1, n2 = S1 * b1 + S2 * b2, S2 * b1 - S1 * b2
    return [zero + a1 + a2, m1 + n1, m2 + n2, m2 - n2, m1 - n1]


def five_complex(re, im, kernel):
    r0, ra1, ra2, rb1, rb2 = five_parts(re)
    i0, ia1, ia2, ib1, ib2 = five_parts(im)
    r = [kernel[0] * r0, kernel[1] * (ra1 + ib1), kernel[2] * (ra2 + ib2), kernel[3] * (ra2 - ib2), kernel[4] * (ra1 - ib1)]
    i = [kernel[0] * i0, kernel[1] * (ia1 - rb1), kernel[2] * (ia2 - rb2), kernel[3] * (ia2 + rb2), kernel[4] * (ia1 + rb1)]
    r0, ra1, ra2, rb1, rb2 = five_parts(r)
    i0, ia1, ia2, ib1, ib2 = five_parts(i)
    return (
        [r0, ra1 - ib1, ra2 - ib2, ra2 + ib2, ra1 + ib1],
        [i0, ia1 + rb1, ia2 + rb2, ia2 - rb2, ia1 - rb1],
    )


def times(table, data):
    high = data.astype(BF16)
    low = (data - high.astype(F32)).astype(BF16)
    stacked = jnp.concatenate([high, low, high], axis=0)
    return lax.dot_general(table, stacked, (((1,), (0,)), ((), ())), preferred_element_type=F32)


def piece(data, index):
    return data[:, LANES * index : LANES * (index + 1)]


def forwards(table_y, table_to, there, turned):
    fill = jnp.zeros((LANES - N, LANES), F32)

    def forward_y(a, b, first, group):
        start = group * PLANES
        density = jnp.concatenate([a[start + i] * b[start + i] for i in range(PLANES)], axis=1)
        along_y = times(table_y[...], density)
        for i in range(PLANES):
            turned[first + start + i] = jnp.concatenate([piece(along_y, i), fill], axis=0).T

    def forward_z(group):
        start = group * PLANES
        rows = [
            jnp.concatenate(
                [
                    turned[start + j // 2, LOW * (j % 2) : LOW * (j % 2) + LOW],
                    turned[start + 4, HIGH * j : HIGH * (j + 1)],
                ],
                axis=0,
            )
            for j in range(GROUP)
        ]
        along_z = times(table_to[...], jnp.concatenate(rows, axis=1))
        for j in range(GROUP):
            there[group * GROUP + j] = piece(along_z, j)

    return forward_y, forward_z


def unit_body(ready, near_a, near_b, far_a, far_b, table_y, table_to, table_from, kernel, total, out, done, there, back, mid, turned):
    done[0, 0] = 0
    forward_y, forward_z = forwards(table_y, table_to, there, turned)

    def plane_at(x):
        return (there if ready is None or x >= HALF else ready).at[x]

    def middle(group, kernel_group):
        rows = pl.ds(pl.multiple_of(group * GROUP, GROUP), GROUP)
        for n2 in range(5):
            for k1, (re, im) in enumerate(real_transform([plane_at(point(n1, n2))[rows, :] for n1 in range(16)])):
                mid[2 * k1, n2] = re
                if im is not None:
                    mid[2 * k1 + 1, n2] = im
        for k1 in range(9):
            scale = [kernel[kernel_group, frequency(k1, k2)] for k2 in range(5)]
            re = [mid[2 * k1, n2] for n2 in range(5)]
            if k1 in (0, 8):
                re = five_real(re, scale)
            else:
                re, im = five_complex(re, [mid[2 * k1 + 1, n2] for n2 in range(5)], scale)
                for n2 in range(5):
                    mid[2 * k1 + 1, n2] = im[n2]
            for n2 in range(5):
                mid[2 * k1, n2] = re[n2]
        for n2 in range(5):
            spectrum = [(mid[2 * k1, n2], None if k1 in (0, 8) else mid[2 * k1 + 1, n2]) for k1 in range(9)]
            for n1, value in enumerate(real_inverse(spectrum)):
                if point(n1, n2) < HALF:
                    back[point(n1, n2), rows, :] = value

    def backward_z(group):
        rows = [back[group * GROUP + j] for j in range(GROUP)]
        along_z = times(table_from[...], jnp.concatenate(rows, axis=1))
        parts = [piece(along_z, j) for j in range(GROUP)]
        packed = [jnp.concatenate([parts[2 * i][:LOW], parts[2 * i + 1][:LOW]], axis=0) for i in range(4)]
        packed.append(jnp.concatenate([part[LOW:] for part in parts], axis=0))
        for i, plane in enumerate(packed):
            turned[group * PLANES + i] = plane.T

    def backward_y(group):
        start = group * PLANES
        planes = jnp.concatenate([turned[start + i, :N] for i in range(PLANES)], axis=1)
        potential = times(table_y[...], planes)
        for i in range(PLANES):
            term = piece(potential, i) * near_b[start + i]
            out[start + i] = term if total is None else total[start + i] + term

    for group in range(GROUPS):
        if ready is None:
            forward_y(near_a, near_b, 0, group)
        forward_y(far_a, far_b, GROUPS * PLANES, group)
    for group in range(0 if ready is None else GROUPS, 2 * GROUPS):
        forward_z(group)

    @functools.partial(pl.loop, 0, 2 * GROUPS, unroll=5)()
    def _(group):
        middle(group, jnp.where(group > GROUPS, group - GROUPS, group))

    for group in range(GROUPS):
        backward_z(group)
    for group in range(GROUPS):
        backward_y(group)


def unit(a, b, constants, after, total=None, waits=(), pick=None, ready=None):
    operands = [a[0], b[0], a[1], b[1], *constants]

    def body(order, *refs):
        refs = list(refs[len(waits) :])
        near_ready = None if ready is None else refs.pop(0)
        if pick is not None:
            x, y, picked = refs.pop(0), refs.pop(0), refs.pop(len(operands) + (total is not None) + 2)
            copy_chosen(pick[0], x, y, picked)
        ins, rest = refs[: len(operands)], refs[len(operands) :]
        if total is None:
            unit_body(near_ready, *ins, None, *rest)
        else:
            unit_body(near_ready, *ins, *rest)

    here = pl.BlockSpec(memory_space=pltpu.VMEM)
    scalar = pl.BlockSpec(memory_space=pltpu.SMEM)
    operands_all = (*(() if ready is None else (ready,)), *(() if pick is None else pick[1:]), *operands, *(() if total is None else (total,)))
    return pl.pallas_call(
        body,
        in_specs=[scalar] + [pl.BlockSpec(memory_space=pl.ANY)] * len(waits) + [here] * len(operands_all),
        out_specs=(here, scalar) + (here,) * (pick is not None),
        out_shape=(jax.ShapeDtypeStruct(PACKED, F32), jax.ShapeDtypeStruct((1, 1), jnp.int32))
        + (jax.ShapeDtypeStruct(PACKED, F32),) * (pick is not None),
        scratch_shapes=[
            pltpu.VMEM((N, N, LANES), F32),
            pltpu.VMEM((HALF, N, LANES), F32),
            pltpu.VMEM((17, 5, GROUP, LANES), F32),
            pltpu.VMEM((2 * GROUPS * PLANES, LANES, LANES), F32),
        ],
        compiler_params=pltpu.CompilerParams(vmem_limit_bytes=20 * 2**20),
        cost_estimate=pl.CostEstimate(flops=1, bytes_accessed=1, transcendentals=0),
        name="unit",
    )(after, *waits, *operands_all)


def ahead_body(a, a_2, b, table_y, table_to, out, out_2, turned, turned_2):
    steps = [forwards(table_y, table_to, out, turned), forwards(table_y, table_to, out_2, turned_2)]
    for group in range(GROUPS):
        steps[0][0](a, b, 0, group)
        steps[1][0](a_2, b, 0, group)
    for group in range(GROUPS):
        steps[0][1](group)
        steps[1][1](group)


def ahead(a, a_2, b, constants):
    here = pl.BlockSpec(memory_space=pltpu.VMEM)
    return pl.pallas_call(
        ahead_body,
        in_specs=[here] * 5,
        out_specs=(here, here),
        out_shape=(jax.ShapeDtypeStruct((HALF, N, LANES), F32),) * 2,
        scratch_shapes=[pltpu.VMEM((GROUPS * PLANES, LANES, LANES), F32)] * 2,
        compiler_params=pltpu.CompilerParams(vmem_limit_bytes=16 * 2**20),
        cost_estimate=pl.CostEstimate(flops=1, bytes_accessed=1, transcendentals=0),
        name="ahead",
    )(a, a_2, b, constants[0], constants[1])


def copy_chosen(places, a, b, out):
    place = lax.axis_index("band")
    takes = functools.reduce(jnp.logical_or, [place == p for p in places])

    @pl.when(takes)
    def _():
        @pl.loop(0, GROUPS * PLANES)
        def _(plane):
            out[plane] = a[plane]

    @pl.when(jnp.logical_not(takes))
    def _():
        @pl.loop(0, GROUPS * PLANES)
        def _(plane):
            out[plane] = b[plane]


def choose_body(places, order, a, b, out):
    copy_chosen(places, a, b, out)


def choose(places, a, b, after):
    here = pl.BlockSpec(memory_space=pltpu.VMEM)
    return pl.pallas_call(
        functools.partial(choose_body, places),
        in_specs=[pl.BlockSpec(memory_space=pltpu.SMEM), here, here],
        out_specs=here,
        out_shape=jax.ShapeDtypeStruct(PACKED, F32),
        compiler_params=pltpu.CompilerParams(vmem_limit_bytes=8 * 2**20),
        cost_estimate=pl.CostEstimate(flops=1, bytes_accessed=1, transcendentals=0),
        name="choose",
    )(after, a, b)


def pack_body(data, out):
    lane = lax.broadcasted_iota(jnp.int32, (N, LANES), 1)
    pad = jnp.zeros((N, LANES - N), F32)

    @pl.loop(0, GROUPS)
    def _(group):
        last = None
        for i in range(4):
            pair = [jnp.concatenate([data[group * GROUP + 2 * i + h], pad], axis=1) for h in range(2)]
            out[group * PLANES + i] = jnp.where(lane < LOW, pair[0], pltpu.roll(pair[1], LOW, 1))
            for h in range(2):
                place = HIGH * (2 * i + h)
                moved = pltpu.roll(pair[h], (place - LOW) % LANES, 1) if place != LOW else pair[h]
                last = moved if last is None else jnp.where(lane >= place, moved, last)
        out[group * PLANES + 4] = last


def pack(data):
    return pl.pallas_call(
        pack_body,
        out_shape=jax.ShapeDtypeStruct(PACKED, F32),
        compiler_params=pltpu.CompilerParams(vmem_limit_bytes=16 * 2**20),
        name="pack",
    )(data)


def unpack_body(total, returned, theirs, out, held, sems):
    lane = lax.broadcasted_iota(jnp.int32, (N, LANES), 1)
    copies = []
    for group in range(GROUPS):
        start = group * PLANES
        planes = [total[start + i] + returned[start + i] + theirs[start + i] for i in range(PLANES)]
        for j in range(GROUP):
            low = planes[j // 2] if j % 2 == 0 else pltpu.roll(planes[j // 2], LOW, 1)
            place = HIGH * j
            high = pltpu.roll(planes[4], (LOW - place) % LANES, 1) if place != LOW else planes[4]
            held[group, j] = jnp.where(lane < LOW, low, high)[:, :N]
        copies.append(pltpu.make_async_copy(held.at[group], out.at[pl.ds(group * GROUP, GROUP)], sems.at[group]))
        copies[-1].start()
    for copy in copies:
        copy.wait()


def unpack_sum(total, returned, theirs):
    return pl.pallas_call(
        unpack_body,
        in_specs=[pl.BlockSpec(memory_space=pltpu.VMEM)] * 3,
        out_specs=pl.BlockSpec(memory_space=pltpu.HBM),
        out_shape=jax.ShapeDtypeStruct((HALF, N, N), F32),
        scratch_shapes=[pltpu.VMEM((GROUPS, GROUP, N, N), F32), pltpu.SemaphoreType.DMA((GROUPS,))],
        compiler_params=pltpu.CompilerParams(vmem_limit_bytes=16 * 2**20),
        name="unpack_sum",
    )(total, returned, theirs)


def shards(orbitals):
    bands = lax.axis_size("band")
    half = bands // 2
    sides = [1 if b % 2 else -1 for b in range(bands)]

    def sources(distance):
        return [(b + distance * sides[b]) % bands for b in range(bands)]

    def takers(distance):
        return [b for b, source in enumerate(sources(distance)) if b // half != source // half]

    def from_place(data, distance):
        return lax.ppermute(data, "band", [(source, b) for b, source in enumerate(sources(distance))])

    def from_half(data, distance):
        return lax.ppermute(data, "band", [(b // half * half + source % half, b) for b, source in enumerate(sources(distance))])

    def far_route(distance):
        route = []
        for b, source in enumerate(sources(distance)):
            for slab in range(2):
                route.append((2 * source + (1 - slab if b in takers(distance) else slab), 2 * b + slab))
        return route

    def swapped_halves(data, distance):
        return lax.ppermute(data, "band", [((b + half) % bands, b) for b in takers(distance)])

    def givers(distance):
        return [sources(distance)[b] for b in takers(distance)]

    def other_core(data):
        return from_place(data, -1)

    constants = tuple(jnp.asarray(t) for t in (*tables(), screened_kernel()))
    near = pack(orbitals[0])
    far = lax.ppermute(near, "grid", [(0, 1), (1, 0)])
    m2_half = from_half(near, -2)
    p2_half = from_half(near, 2)
    far, m2_half, p2_half = lax.optimization_barrier((far, m2_half, p2_half))
    own = (near, far)
    first = jnp.zeros((1, 1), jnp.int32)
    m2_far = lax.ppermute(choose(givers(-2), near, far, first), ("band", "grid"), far_route(-2))
    m1 = (other_core(near), other_core(far))
    m2_swapped = swapped_halves(m2_half, -2)
    total, after, p2_sent = unit(own, m1, constants, first, pick=(givers(2), near, far))
    p2_far = lax.ppermute(p2_sent, ("band", "grid"), far_route(2))
    p2_half, after = lax.optimization_barrier((p2_half, after))
    p2_swapped = swapped_halves(p2_half, 2)
    m2_near = choose(takers(-2), m2_swapped, m2_half, after)
    p1_near = other_core(m2_near)
    own_m2, m1_m2 = ahead(near, m1[0], m2_near, constants)
    m2_far, p1_near, own_m2, m1_m2, after = lax.optimization_barrier((m2_far, p1_near, own_m2, m1_m2, after))
    m2 = (m2_near, m2_far)
    p1 = (p1_near, other_core(m2_far))
    total, after = unit(own, m2, constants, after, total, ready=own_m2)
    lent, after = unit(m2, p1, constants, after)
    returned = from_place(lent, 2)
    partner, after, p2_near = unit(
        m1, m2, constants, after, waits=(p2_far,), pick=(takers(2), p2_swapped, p2_half), ready=m1_m2
    )
    p2 = (p2_near, p2_far)
    partner, after = unit(m1, p2, constants, after, partner)
    theirs = other_core(partner)
    total, after = unit(own, p2, constants, after, total, waits=(returned,))
    return unpack_sum(total, returned, theirs)[None]


def solution(mesh):
    spec = P("band", "grid", None, None)
    return jax.shard_map(shards, mesh=mesh, in_specs=(spec,), out_specs=spec, check_vma=False)
```
